128 devices in a mesh: rows: 32 (over y, z, core), mp: 4 (over x).
Axes of the slice: x: 4, y: 4, z: 4, core: 2. Of those that a mesh axis runs over, the one named last changes fastest.
Arguments:
- calib: bfloat16 [2048, 8192], P('rows', 'mp'), may hold values from -40 to 40
- weight: bfloat16 [8192, 8192], P('rows', 'mp'), may hold values from -6 to 6
- inverse_factor: float32 [8192, 8192], P('rows', 'mp'), may hold values from -10 to 12, as said below
- pruned_blocks: int32 [7], replicated, may hold values from 0 to 63, as said below
Outputs:
- pruned_weight: bfloat16 [8192, 8192], P('rows', 'mp')
- next_gram: float32 [8192, 8192], P('rows', 'mp')
The draws below stay inside these ranges and needn't reach their ends.
Inputs may be any that keep to these rules, and one draw needn't show every extreme that they name: `pruned_blocks`: 7 distinct block numbers in any order; block b holds rows b * 128 to b * 128 + 127. `inverse_factor`: symmetric and positive definite.
All inputs are finite; a program needn't handle non-finite values.
Results may differ from the reference program's by a relative error of at most 0.0095.
Values may be sent and summed in bfloat16 or wider, within the bound.
No kernel may reach another device: no remote copies, remote signals or barrier semaphores. Data moves between devices by JAX's collectives and lax.ppermute only.
A program may use at most 128 MiB of HBM per device.

```python
import jax
import jax.numpy as jnp
from jax import lax

D = 8192
BLOCK = 128
NB = 7
TOKENS = 2048


def draw_calib(key, part):
    first, second, third = jax.random.split(jax.random.fold_in(key, 31), 3)
    row_scale = jnp.exp(jax.random.uniform(first, (TOKENS, 1), jnp.float32, jnp.log(0.3), jnp.log(3.0)))
    col_scale = jnp.exp(jax.random.uniform(second, (1, D), jnp.float32, jnp.log(0.5), jnp.log(2.0)))
    values = jax.random.normal(third, (TOKENS, D), jnp.float32)
    return jnp.clip(values * row_scale * col_scale, -40.0, 40.0).astype(jnp.bfloat16)


def draw_inverse_factor(key, part):
    first, second, third = jax.random.split(jax.random.fold_in(key, 11), 3)
    factor_rank = max(NB * BLOCK // 4, 4)
    coeff = 0.003 / jnp.sqrt(2.0 * D)
    noise = jax.random.normal(first, (D, D), jnp.float32)
    diagonal = jnp.exp(jax.random.uniform(second, (D,), jnp.float32, jnp.log(0.02), jnp.log(2.0)))
    loadings = jnp.clip(jax.random.normal(third, (D, factor_rank), jnp.float32), -3.0, 3.0)
    noise = jnp.clip(noise, -6.0, 6.0)
    shared = jnp.dot(loadings, loadings.T, precision=lax.Precision.HIGHEST) * (1.0 / factor_rank)
    shared = 0.5 * (shared + shared.T)
    return (noise + noise.T) * coeff + shared + jnp.diag(diagonal)


def draw_pruned_blocks(key, part):
    first, second = jax.random.split(jax.random.fold_in(key, 5), 2)
    inner = jax.random.permutation(first, D // BLOCK - 2)[:NB - 2].astype(jnp.int32) + 1
    ends = jnp.array([0, D // BLOCK - 1], dtype=jnp.int32)
    blocks = jnp.concatenate([ends, inner])
    order = jax.random.permutation(second, NB)
    return blocks[order].astype(jnp.int32)


def levels(key, extent, shards, smallest, high):
    def one(axis_at, parts):
        draws = jax.random.uniform(jax.random.fold_in(jax.random.fold_in(key, 6), axis_at), (parts,), jnp.float32, smallest / len(shards), high / len(shards))
        return jnp.repeat(jnp.exp(draws), extent[axis_at] // parts).reshape((-1,) + (1,) * (len(extent) - axis_at - 1))

    level = one(*shards[0])
    for cut in shards[1:]:
        level = level * one(*cut)
    return level


def scatter_about(own_key, extent, width, reach, cuts=(), kind=jnp.bfloat16):
    values = jax.random.normal(own_key, extent, jnp.float32) * width
    if len(cuts) > 0:
        values = levels(own_key, extent, cuts, -0.22, 0.18) * values
    return jnp.clip(values, min=-reach, max=reach).astype(kind)


def setup_inputs(seed: int = 0) -> dict:
    streams_of = jax.random.split(jax.random.key(seed), 5)
    return {
        "calib": draw_calib(jax.random.fold_in(streams_of[4], 71), 0),
        "weight": scatter_about(streams_of[1], (D, D), 1.0, 6.0, ((0, 32), (1, 4))),
        "inverse_factor": draw_inverse_factor(jax.random.fold_in(streams_of[4], 71), 0),
        "pruned_blocks": draw_pruned_blocks(jax.random.fold_in(streams_of[4], 71), 0),
    }


def spd_solve(chol_lower, right_side):
    forward = lax.linalg.triangular_solve(chol_lower, right_side, left_side=True, lower=True)
    return lax.linalg.triangular_solve(chol_lower, forward, left_side=True, lower=True, transpose_a=True)

def reference(calib, weight, inverse_factor, pruned_blocks):
    row_numbers = (pruned_blocks[:, None] * BLOCK + jnp.arange(BLOCK, dtype=jnp.int32)[None, :]).reshape(-1).astype(jnp.int32)
    columns = jnp.take(inverse_factor, row_numbers, axis=1)
    square = jnp.take(columns, row_numbers, axis=0)
    kept_rows = jnp.take(weight, row_numbers, axis=0).astype(jnp.float32)
    chol_lower = jnp.linalg.cholesky(square)
    solved = spd_solve(chol_lower, kept_rows)
    update = jnp.dot(columns, solved, precision=lax.Precision.HIGHEST)
    block_ids = jnp.arange(D, dtype=jnp.int32) // BLOCK
    kept_mask = 1.0 - jnp.any(block_ids[:, None] == pruned_blocks[None, :], axis=1).astype(jnp.float32)
    pruned_weight = ((weight.astype(jnp.float32) - update) * kept_mask[:, None]).astype(jnp.bfloat16)
    projected = jnp.dot(calib.astype(jnp.float32), pruned_weight.T.astype(jnp.float32), preferred_element_type=jnp.float32)
    outputs = (projected * float(D) ** (-0.5)).astype(jnp.bfloat16)
    next_gram = jnp.dot(outputs.T.astype(jnp.float32), outputs.astype(jnp.float32), preferred_element_type=jnp.float32) / TOKENS
    return (pruned_weight, next_gram)
```

```python
import jax
import jax.numpy as jnp
from jax import lax
from jax.experimental import pallas as pl
from jax.experimental.pallas import tpu as pltpu
from jax.sharding import PartitionSpec as P

BLOCK = 128
NB = 7
F32 = jnp.float32


def dot_full(a, b):
    return lax.dot_general(a, b, (((1,), (0,)), ((), ())), precision=lax.Precision.HIGHEST,
                           preferred_element_type=F32)


def dot_full_t(a, b):
    return lax.dot_general(a, b, (((1,), (1,)), ((), ())), precision=lax.Precision.HIGHEST,
                           preferred_element_type=F32)


def spread(v, shape=(8, BLOCK)):
    return jnp.broadcast_to(v, shape)


def invert_two(a, b, d):
    r = 1.0 / (a * d - b * b)
    return d * r, -b * r, a * r


def invert_four(e):
    p00, p01, p11 = invert_two(e[0][0], e[0][1], e[1][1])
    b00, b01, b10, b11 = e[0][2], e[0][3], e[1][2], e[1][3]
    w00 = p00 * b00 + p01 * b10
    w01 = p00 * b01 + p01 * b11
    w10 = p01 * b00 + p11 * b10
    w11 = p01 * b01 + p11 * b11
    s00 = e[2][2] - (b00 * w00 + b10 * w10)
    s01 = e[2][3] - (b00 * w01 + b10 * w11)
    s11 = e[3][3] - (b01 * w01 + b11 * w11)
    t00, t01, t11 = invert_two(s00, s01, s11)
    v00 = w00 * t00 + w01 * t01
    v01 = w00 * t01 + w01 * t11
    v10 = w10 * t00 + w11 * t01
    v11 = w10 * t01 + w11 * t11
    q00 = p00 + v00 * w00 + v01 * w01
    q01 = p01 + v00 * w10 + v01 * w11
    q11 = p11 + v10 * w10 + v11 * w11
    return [
        [q00, q01, -v00, -v01],
        [q01, q11, -v10, -v11],
        [-v00, -v10, t00, t01],
        [-v01, -v11, t01, t11],
    ]


def invert_block(load, lane, sub):
    groups = [load(g) for g in range(BLOCK // 8)]
    for k in range(0, BLOCK, 4):
        home, base = k // 8, k % 8
        cols = [[spread(groups[g][:, k + t:k + t + 1]) for t in range(4)] for g in range(BLOCK // 8)]
        rows = [spread(groups[home][base + t:base + t + 1, :]) for t in range(4)]
        e = [[spread(cols[home][t][base + s:base + s + 1, :]) if s <= t else None for t in range(4)]
             for s in range(4)]
        q = invert_four(e)
        rows = [jnp.where(lane == k + t, 1.0, jnp.where((lane >= k) & (lane < k + 4), 0.0, rows[t]))
                for t in range(4)]
        new = [q[t][0] * rows[0] + q[t][1] * rows[1] + (q[t][2] * rows[2] + q[t][3] * rows[3])
               for t in range(4)]
        keep = (lane < k) | (lane >= k + 4)
        out = []
        for g in range(BLOCK // 8):
            v = jnp.where(keep, groups[g], 0.0)
            v = (v - cols[g][0] * new[0] - cols[g][1] * new[1]) - (cols[g][2] * new[2] + cols[g][3] * new[3])
            if g == home:
                for t in range(4):
                    v = jnp.where(sub == base + t, new[t], v)
            out.append(v)
        groups = out
    return groups


def solve_kernel(coord_ref, *refs):
    pieces, (columns_ref, gain_ref, work, pivots) = refs[:2 * CHIPS], refs[2 * CHIPS:]
    n = NB * BLOCK
    x, core = coord_ref[0], coord_ref[1]
    for step in range(CHIPS):
        quarter = lax.rem(x - step + CHIPS, CHIPS)
        for other in range(2):
            place = quarter * 32 + (core if other == 0 else 1 - core) * 16
            for slot in range(NB):
                start = pl.multiple_of(slot * BLOCK + place, 16)
                for turn in range(TURNS):
                    col = (slot + turn) % NB
                    work[pl.ds(start, 16), col * BLOCK:(col + 1) * BLOCK] = pieces[2 * step + other][
                        slot, :, turn * BLOCK:(turn + 1) * BLOCK]
    for slot in range(NB):
        for turn in range(1, TURNS):
            col = (slot + turn) % NB
            work[col * BLOCK:(col + 1) * BLOCK, slot * BLOCK:(slot + 1) * BLOCK] = work[
                slot * BLOCK:(slot + 1) * BLOCK, col * BLOCK:(col + 1) * BLOCK].T
    work[n:, :] = columns_ref[...]
    lane = lax.broadcasted_iota(jnp.int32, (8, BLOCK), 1)
    sub = lax.broadcasted_iota(jnp.int32, (8, BLOCK), 0)
    for k in range(NB):
        lo, hi = k * BLOCK, (k + 1) * BLOCK
        groups = invert_block(lambda g: work[lo + g * 8:lo + g * 8 + 8, lo:hi], lane, sub)
        for g in range(BLOCK // 8):
            pivots[lo + g * 8:lo + g * 8 + 8, :] = groups[g]
        lower = dot_full(work[hi:, lo:hi], pivots[lo:hi, :])
        if k + 1 < NB:
            work[hi:, hi:] -= dot_full(lower, work[lo:hi, hi:])
        work[hi:, lo:hi] = lower
    gain_ref[:, n - BLOCK:] = work[n:, n - BLOCK:].astype(gain_ref.dtype)
    for k in range(NB - 2, -1, -1):
        lo, hi = k * BLOCK, (k + 1) * BLOCK
        work[n:, lo:hi] -= dot_full(work[n:, hi:], work[hi:n, lo:hi])
        gain_ref[:, lo:hi] = work[n:, lo:hi].astype(gain_ref.dtype)


def solve(coords, pieces, columns):
    n = NB * BLOCK
    extra = columns.shape[0]
    return pl.pallas_call(
        solve_kernel,
        out_shape=jax.ShapeDtypeStruct((extra, n), jnp.bfloat16),
        in_specs=[pl.BlockSpec(memory_space=pltpu.SMEM)]
        + [pl.BlockSpec(memory_space=pltpu.VMEM)] * (len(pieces) + 1),
        out_specs=pl.BlockSpec(memory_space=pltpu.VMEM),
        scratch_shapes=[pltpu.VMEM((n + extra, n), F32), pltpu.VMEM((n, BLOCK), F32)],
        compiler_params=pltpu.CompilerParams(vmem_limit_bytes=40 * 2**20),
        cost_estimate=pl.CostEstimate(flops=6 * 10**10, bytes_accessed=10**7, transcendentals=0),
    )(coords, *pieces, columns)


CHIPS = 4
TURNS = NB // 2 + 1
AXES = ("rows", "mp")


def device_id(x, y, z, c):
    return ((y * CHIPS + z) * 2 + c) * CHIPS + x


def permute(value, target):
    pairs = []
    for x in range(CHIPS):
        for y in range(CHIPS):
            for z in range(CHIPS):
                for c in range(2):
                    pairs.append((device_id(x, y, z, c), device_id(*target(x, y, z, c))))
    return lax.ppermute(value, AXES, pairs)


def shifted(value, axis, step):
    def target(x, y, z, c):
        at = [x, y, z, c]
        at[axis] = (at[axis] + step) % CHIPS
        return at

    return permute(value, target)


def partner(value):
    return permute(value, lambda x, y, z, c: (x, y, z, 1 - c))


def pick(stack, index):
    return lax.dynamic_index_in_dim(stack, index, 0, keepdims=False)


def gathered(value, axis):
    return [value] + [shifted(value, axis, step) for step in range(1, CHIPS)]


def exchanged(stack, axis, here):
    return [pick(stack, here)] + [
        shifted(pick(stack, lax.rem(here + step, CHIPS)), axis, step) for step in range(1, CHIPS)
    ]


def in_order(parts, here):
    stack = jnp.stack(parts + parts[:0])
    order = [pick(stack, lax.rem(here - place + CHIPS, CHIPS)) for place in range(CHIPS)]
    return jnp.stack(order)


def shards(calib, weight, inverse_factor, pruned_blocks):
    rows_dev, width_dev = weight.shape
    full_width = width_dev * CHIPS
    r = lax.axis_index("rows")
    x = lax.axis_index("mp")
    y, z, core = r // 8, (r // 2) % CHIPS, r % 2
    col_start = x * width_dev
    starts = pruned_blocks * BLOCK
    half_width = width_dev // 2
    tokens_dev = calib.shape[0]
    token_count = tokens_dev * 32

    col_pieces = []
    for slot in range(NB):
        offset = starts[slot] - col_start
        inside = ((offset >= 0) & (offset < width_dev)).astype(F32)
        clamped = jnp.clip(offset, 0, width_dev - BLOCK)
        col_pieces.append(lax.dynamic_slice_in_dim(inverse_factor, clamped, BLOCK, 1) * inside)
    masked = jnp.concatenate(col_pieces, axis=1)
    by_quarter = masked.reshape(2, CHIPS, 32, NB * BLOCK).transpose(1, 0, 2, 3)
    got = exchanged(by_quarter, 0, x)
    columns = (got[0] + got[1]) + (got[2] + got[3])

    doubled = jnp.concatenate([columns, columns[:, :, :(TURNS - 1) * BLOCK]], axis=2)
    turned = []
    for half in range(2):
        slot = jnp.argmax(pruned_blocks == 2 * r + half).astype(jnp.int32)
        turned.append(lax.dynamic_slice_in_dim(doubled[half], slot * BLOCK, TURNS * BLOCK, 1))
    turned = jnp.stack(turned).reshape(2, 2, 16, TURNS * BLOCK).transpose(1, 0, 2, 3)
    chip_blocks = jnp.stack([pick(turned, core), partner(pick(turned, 1 - core))])
    line = jnp.stack(gathered(chip_blocks, 2)).reshape(16, 16, TURNS * BLOCK)
    slot_y, slot_z = pruned_blocks // 16, (pruned_blocks // 4) % CHIPS
    slot_core, slot_half = (pruned_blocks // 2) % 2, pruned_blocks % 2
    back = lax.rem(z - slot_z + CHIPS, CHIPS)
    apart = (slot_core != core).astype(jnp.int32)
    mine = slot_y == y
    at = back * 4 + apart * 2 + slot_half
    chosen = jnp.stack([pick(line, at[slot]) * mine[slot].astype(F32) for slot in range(NB)])
    parts = gathered(chosen, 1)
    total = (parts[0] + parts[1]) + (parts[2] + parts[3])
    pieces = []
    for piece in gathered(total, 0):
        pieces += [piece, partner(piece)]

    halves = weight.reshape(rows_dev, 2, half_width)
    own_half = lax.dynamic_index_in_dim(halves, core, 1, keepdims=False)
    other_half = partner(lax.dynamic_index_in_dim(halves, 1 - core, 1, keepdims=False))
    chip_weight = jnp.stack([own_half, other_half])
    cut = chip_weight.reshape(4, CHIPS, 32, half_width).transpose(1, 0, 2, 3)
    rows_line = jnp.stack(exchanged(cut, 2, z)).reshape(16, 32, half_width)
    rows_chosen = jnp.stack(
        [jnp.where(mine[slot], pick(rows_line, at[slot]), 0) for slot in range(NB)]
    )
    parts = gathered(rows_chosen, 1)
    rows_quarter = (parts[0] + parts[1]) + (parts[2] + parts[3])
    kept = in_order(gathered(rows_quarter, 2), z).transpose(1, 0, 2, 3).reshape(NB * BLOCK, half_width)

    plane = [[core_at + 2 * chip for chip in range(16)] for core_at in range(2)]
    tokens = lax.all_gather(calib, "rows", axis=0, tiled=True, axis_index_groups=plane)

    coords = jnp.stack([x, core]).astype(jnp.int32)
    gain = solve(coords, pieces, columns.reshape(2 * 32, NB * BLOCK))

    gain_rows = in_order(gathered(gain.reshape(2, 32, NB * BLOCK), 0), x)
    gain_rows = gain_rows.transpose(1, 0, 2, 3).reshape(rows_dev, NB * BLOCK)
    gain_chip = jnp.concatenate([gain_rows, partner(gain_rows)], axis=0)
    update = jnp.dot(gain_chip, kept, preferred_element_type=F32)
    row = jnp.arange(rows_dev, dtype=jnp.int32)
    block_ids = jnp.concatenate([r * rows_dev + row, (r + 1 - 2 * core) * rows_dev + row]) // BLOCK
    kept_mask = jnp.logical_not(jnp.any(block_ids[:, None] == pruned_blocks[None, :], axis=1))
    weight_chip = chip_weight.reshape(2 * rows_dev, half_width)
    pruned_chip = jnp.where(
        kept_mask[:, None], weight_chip.astype(F32) - update, 0.0
    ).astype(jnp.bfloat16)
    pruned_other = partner(pruned_chip).reshape(2, rows_dev, half_width)[::-1].reshape(
        2 * rows_dev, half_width)
    left = jnp.where(core == 0, pruned_chip, pruned_other)
    right = jnp.where(core == 0, pruned_other, pruned_chip)
    both = jnp.concatenate([left, right], axis=1)
    pruned_weight = both[:rows_dev]

    partial_value = lax.dot_general(
        tokens, both, (((1,), (1,)), ((), ())), preferred_element_type=F32
    ).reshape(CHIPS, -1, 2 * rows_dev)
    out_scale = float(full_width) ** (-0.5)
    narrow = partial_value.astype(jnp.bfloat16)
    summed = pick(partial_value, x)
    for step in range(1, CHIPS):
        summed = summed + shifted(pick(narrow, lax.rem(x + step, CHIPS)), 0, step).astype(F32)
    chunk = (summed * out_scale).astype(jnp.bfloat16)
    chunk = chunk.reshape(-1, 2, rows_dev)
    chunk = jnp.where(core == 0, chunk, chunk[:, ::-1]).reshape(-1, 2 * rows_dev)

    own = in_order(gathered(chunk, 0), x)
    crossed = permute(chunk, lambda x, y, z, c: (y, x, z, c))
    others = lax.all_gather(crossed, "rows", axis=0, axis_index_groups=plane)
    others = others.reshape((CHIPS, CHIPS) + chunk.shape)
    gram = jnp.einsum("tkf,tzkg->fzg", own, others, preferred_element_type=F32)
    gram = gram.reshape(2, rows_dev, width_dev)
    gram_block = (pick(gram, core) + partner(pick(gram, 1 - core))) / token_count
    return (pruned_weight, gram_block)


def solution(mesh):
    return jax.shard_map(
        shards,
        mesh=mesh,
        in_specs=(P("rows", "mp"), P("rows", "mp"), P("rows", "mp"), P()),
        out_specs=(P("rows", "mp"), P("rows", "mp")),
        check_vma=False,
    )
```

```python
import jax
import jax.numpy as jnp
from jax import lax
from jax.experimental import pallas as pl
from jax.experimental.pallas import tpu as pltpu
from jax.sharding import PartitionSpec as P

BLOCK = 128
NB = 7
F32 = jnp.float32
GROUPS = BLOCK // 8
PANEL = 4


def dot_full(a, b):
    return lax.dot_general(
        a, b, (((1,), (0,)), ((), ())), precision=lax.Precision.HIGHEST, preferred_element_type=F32
    )


def dot_once(a, b):
    return lax.dot_general(a, b, (((1,), (0,)), ((), ())), preferred_element_type=F32)


def halves(a):
    high = a.astype(jnp.bfloat16)
    return high, (a - high.astype(F32)).astype(jnp.bfloat16)


def dot_split(a, b):
    (a_high, a_low), (b_high, b_low) = halves(a), halves(b)
    return dot_once(a_high, b_high) + (dot_once(a_high, b_low) + dot_once(a_low, b_high))


def spread(v):
    return jnp.broadcast_to(v, (8, BLOCK))


def lane_of(v, k):
    return jnp.take_along_axis(v, jnp.full((8, BLOCK), k, jnp.int32), axis=1)


def tree(terms):
    while len(terms) > 1:
        terms = [
            terms[i] + terms[i + 1] if i + 1 < len(terms) else terms[i]
            for i in range(0, len(terms), 2)
        ]
    return terms[0]


def invert_small(e):
    n = len(e)
    if n == 2:
        a, b, d = e[0][0], e[0][1], e[1][1]
        r = 1.0 / (a * d - b * b)
        off = -(b * r)
        return [[d * r, off], [off, a * r]]
    h = n // 2
    p = invert_small([row[:h] for row in e[:h]])
    b = [row[h:] for row in e[:h]]
    w = [[tree([p[i][k] * b[k][j] for k in range(h)]) for j in range(h)] for i in range(h)]
    s = [[None] * h for _ in range(h)]
    for i in range(h):
        for j in range(i, h):
            s[i][j] = s[j][i] = e[h + i][h + j] - tree([b[k][i] * w[k][j] for k in range(h)])
    t = invert_small(s)
    v = [[tree([w[i][k] * t[k][j] for k in range(h)]) for j in range(h)] for i in range(h)]
    q = [[None] * n for _ in range(n)]
    for i in range(h):
        for j in range(h):
            q[h + i][h + j] = t[i][j]
            q[i][h + j] = q[h + j][i] = -v[i][j]
        for j in range(i, h):
            q[i][j] = q[j][i] = p[i][j] + tree([v[i][k] * w[j][k] for k in range(h)])
    return q


def panel_steps(groups, first, lane, sub):
    for home in range(len(groups)):
        k = first + 8 * home
        cols = [[lane_of(group, k + t) for t in range(8)] for group in groups]
        e = [[None] * 8 for _ in range(8)]
        for t in range(8):
            for s in range(t + 1):
                e[s][t] = e[t][s] = spread(cols[home][t][s:s + 1, :])
        q = invert_small(e)
        inside = (lane >= k) & (lane < k + 8)
        rows = [
            jnp.where(lane == k + t, 1.0, jnp.where(inside, 0.0, spread(groups[home][t:t + 1, :])))
            for t in range(8)
        ]
        new = [tree([q[t][i] * rows[i] for i in range(8)]) for t in range(8)]
        out = []
        for g, group in enumerate(groups):
            if g == home:
                v = new[0]
                for t in range(1, 8):
                    v = jnp.where(sub == t, new[t], v)
            else:
                v = jnp.where(inside, 0.0, group) - tree([cols[g][t] * new[t] for t in range(8)])
            out.append(v)
        groups = out
    return groups


def invert_block(groups, lane, sub):
    for first in range(0, GROUPS, PANEL):
        panel = panel_steps(groups[first:first + PANEL], first * 8, lane, sub)
        inside = (lane >= first * 8) & (lane < (first + PANEL) * 8)
        left = jnp.concatenate(groups, axis=0)[:, first * 8:(first + PANEL) * 8]
        change = dot_full(left, jnp.concatenate(panel, axis=0))
        groups = [
            panel[g - first]
            if first <= g < first + PANEL
            else jnp.where(inside, 0.0, groups[g]) - change[g * 8:g * 8 + 8, :]
            for g in range(GROUPS)
        ]
    return groups


CHIPS = 4
TURNS = NB // 2 + 1
AXES = ("rows", "mp")
N = NB * BLOCK
BF16 = jnp.bfloat16
META = 4


def whole(count):
    return [pl.BlockSpec(memory_space=pltpu.VMEM)] * count


SMEM = pl.BlockSpec(memory_space=pltpu.SMEM)
ANY = pl.BlockSpec(memory_space=pl.ANY)


def cost(flops, data):
    return pl.CostEstimate(flops=flops, bytes_accessed=data, transcendentals=0)


def params():
    return pltpu.CompilerParams(vmem_limit_bytes=44 * 2**20)


def shape(dims, dtype):
    return jax.ShapeDtypeStruct(dims, dtype)


def ahead(place, step):
    return lax.rem(place + step, CHIPS)


def behind(place, step):
    return lax.rem(place - step + CHIPS, CHIPS)


def block_number(meta, slot):
    return meta[META + slot]


def columns_kernel(meta, source, *refs):
    outs, buffer, sems = refs[:CHIPS], refs[CHIPS], refs[CHIPS + 1]
    width = source.shape[1]
    inside = []
    for slot in range(NB):
        offset = block_number(meta, slot) * BLOCK - meta[0] * width
        ok = jnp.logical_and(offset >= 0, offset < width)
        inside.append(jnp.where(ok, 1.0, 0.0).astype(F32))
        start = pl.multiple_of(jnp.clip(offset, 0, width - BLOCK), BLOCK)
        pltpu.make_async_copy(source.at[:, pl.ds(start, BLOCK)], buffer.at[slot], sems.at[slot]).start()
    for slot in range(NB):
        pltpu.make_async_copy(source.at[:, pl.ds(0, BLOCK)], buffer.at[slot], sems.at[slot]).wait()
        for step in range(CHIPS):
            quarter = ahead(meta[0], step)
            for half in range(2):
                start = pl.multiple_of(half * BLOCK + quarter * 32, 32)
                outs[step][half, :, slot * BLOCK:(slot + 1) * BLOCK] = (
                    buffer[slot, pl.ds(start, 32), :] * inside[slot]
                )


def pruned_columns(meta, inverse_factor):
    return pl.pallas_call(
        columns_kernel,
        out_shape=[shape((2, 32, N), F32)] * CHIPS,
        in_specs=[SMEM, ANY],
        out_specs=whole(CHIPS),
        scratch_shapes=[
            pltpu.VMEM((NB, inverse_factor.shape[0], BLOCK), F32),
            pltpu.SemaphoreType.DMA((NB,)),
        ],
        compiler_params=params(),
        cost_estimate=cost(10**6, 6 * 10**6),
    )(meta, inverse_factor)


def turn_kernel(meta, a, b, c, d, columns_ref, keep_ref, send_ref, doubled):
    core = meta[3]
    number = (meta[1] * CHIPS + meta[2]) * 2 + core
    for half in range(2):
        total = (a[half] + b[half]) + (c[half] + d[half])
        columns_ref[half * 32:(half + 1) * 32, :] = total
        doubled[half * 32:(half + 1) * 32, :N] = total
        doubled[half * 32:(half + 1) * 32, N:] = total[:, :(TURNS - 1) * BLOCK]
    for half in range(2):
        slot = jnp.int32(0)
        for candidate in range(NB):
            slot = jnp.where(block_number(meta, candidate) == 2 * number + half, candidate, slot)
        lanes = pl.ds(pl.multiple_of(slot * BLOCK, BLOCK), TURNS * BLOCK)
        keep_ref[half] = doubled[pl.ds(pl.multiple_of(half * 32 + core * 16, 16), 16), lanes]
        send_ref[half] = doubled[pl.ds(pl.multiple_of(half * 32 + (1 - core) * 16, 16), 16), lanes]


def turned_rows(meta, parts):
    return pl.pallas_call(
        turn_kernel,
        out_shape=[shape((64, N), F32)] + [shape((2, 16, TURNS * BLOCK), F32)] * 2,
        in_specs=[SMEM] + whole(CHIPS),
        out_specs=whole(3),
        scratch_shapes=[pltpu.VMEM((64, N + (TURNS - 1) * BLOCK), F32)],
        compiler_params=params(),
        cost_estimate=cost(10**6, 2 * 10**6),
    )(meta, *parts)


def source_of(meta, slot):
    block = block_number(meta, slot)
    y, z = lax.div(block, 16), lax.rem(lax.div(block, 4), 4)
    return y, behind(meta[2], z), lax.rem(lax.div(block, 2), 2), lax.rem(block, 2)


def choose_kernel(meta, a, b, c, d, out_ref):
    for slot in range(NB):
        y, step, core, half = source_of(meta, slot)
        apart = jnp.where(core == meta[3], 0, 1)
        out_ref[slot] = jnp.zeros(out_ref.shape[1:], out_ref.dtype)
        for index, part in enumerate((a, b, c, d)):
            @pl.when(jnp.logical_and(y == meta[1], step == index))
            def _(part=part):
                out_ref[slot] = part[apart, half]


def chosen_rows(meta, parts):
    return pl.pallas_call(
        choose_kernel,
        out_shape=shape((NB, 16, TURNS * BLOCK), F32),
        in_specs=[SMEM] + whole(CHIPS),
        out_specs=pl.BlockSpec(memory_space=pltpu.VMEM),
        compiler_params=params(),
        cost_estimate=cost(10**6, 10**6),
    )(meta, *parts)


def solve_kernel(meta, *refs):
    pieces, columns = refs[:2 * CHIPS], refs[2 * CHIPS:3 * CHIPS]
    gain_ref, work = refs[3 * CHIPS:]
    for step in range(CHIPS):
        quarter = behind(meta[0], step)
        for other in range(2):
            place = quarter * 32 + (meta[3] if other == 0 else 1 - meta[3]) * 16
            for slot in range(NB):
                start = pl.multiple_of(slot * BLOCK + place, 16)
                for turn in range(TURNS):
                    col = (slot + turn) % NB
                    work[pl.ds(start, 16), col * BLOCK:(col + 1) * BLOCK] = pieces[2 * step + other][
                        slot, :, turn * BLOCK:(turn + 1) * BLOCK]
        for half in range(2):
            start = pl.multiple_of(N + half * BLOCK + quarter * 32, 32)
            work[pl.ds(start, 32), :] = columns[step][half * 32:(half + 1) * 32, :]
    for slot in range(NB):
        for turn in range(1, TURNS):
            col = (slot + turn) % NB
            work[col * BLOCK:(col + 1) * BLOCK, slot * BLOCK:(slot + 1) * BLOCK] = work[
                slot * BLOCK:(slot + 1) * BLOCK, col * BLOCK:(col + 1) * BLOCK].T
    lane = lax.broadcasted_iota(jnp.int32, (8, BLOCK), 1)
    sub = lax.broadcasted_iota(jnp.int32, (8, BLOCK), 0)
    for k in range(NB):
        lo, hi = k * BLOCK, (k + 1) * BLOCK
        groups = invert_block([work[lo + g * 8:lo + g * 8 + 8, lo:hi] for g in range(GROUPS)], lane, sub)
        pivot = jnp.concatenate(groups, axis=0)
        if k + 1 < NB:
            upper = work[lo:hi, hi:]
            lower = dot_full(work[hi:N, lo:hi], pivot)
            work[hi:N, hi:] -= dot_full(lower, upper)
            work[hi:N, lo:hi] = lower
        gain = dot_split(work[N:, lo:hi], pivot)
        if k + 1 < NB:
            work[N:, hi:] -= dot_split(gain, upper)
        work[N:, lo:hi] = gain
    gain_ref[:, N - BLOCK:] = work[N:, N - BLOCK:].astype(gain_ref.dtype)
    for k in range(NB - 2, -1, -1):
        lo, hi = k * BLOCK, (k + 1) * BLOCK
        work[N:, lo:hi] -= dot_split(work[N:, hi:], work[hi:N, lo:hi])
        gain_ref[:, lo:hi] = work[N:, lo:hi].astype(gain_ref.dtype)


def solve(meta, pieces, columns):
    extra = CHIPS * columns[0].shape[0]
    return pl.pallas_call(
        solve_kernel,
        out_shape=shape((extra, N), BF16),
        in_specs=[SMEM] + whole(3 * CHIPS),
        out_specs=pl.BlockSpec(memory_space=pltpu.VMEM),
        scratch_shapes=[pltpu.VMEM((N + extra, N), F32)],
        compiler_params=params(),
        cost_estimate=cost(6 * 10**10, 10**7),
    )(meta, *pieces, *columns)


def rows_kernel(meta, weight_ref, *refs):
    outs, keep_ref, send_ref = refs[:CHIPS], refs[CHIPS], refs[CHIPS + 1]
    width = weight_ref.shape[1] // 2
    for step in range(CHIPS):
        quarter = ahead(meta[2], step)
        for half in range(2):
            start = pl.multiple_of(half * BLOCK + quarter * 32, 32)
            outs[step][half] = weight_ref[pl.ds(start, 32), :]
    keep_ref[...] = weight_ref[:, pl.ds(pl.multiple_of(meta[3] * width, BLOCK), width)]
    send_ref[...] = weight_ref[:, pl.ds(pl.multiple_of((1 - meta[3]) * width, BLOCK), width)]


def weight_rows(meta, weight):
    rows, width = weight.shape
    return pl.pallas_call(
        rows_kernel,
        out_shape=[shape((2, 32, width), BF16)] * CHIPS + [shape((rows, width // 2), BF16)] * 2,
        in_specs=[SMEM] + whole(1),
        out_specs=whole(CHIPS + 2),
        compiler_params=params(),
        cost_estimate=cost(10**6, 4 * 10**6),
    )(meta, weight)


def choose_weight_kernel(meta, a, b, c, d, keep_ref, send_ref):
    width = keep_ref.shape[2]
    keep_at = pl.ds(pl.multiple_of(meta[3] * width, BLOCK), width)
    send_at = pl.ds(pl.multiple_of((1 - meta[3]) * width, BLOCK), width)
    for slot in range(NB):
        y, step, core, half = source_of(meta, slot)
        mine = jnp.logical_and(y == meta[1], core == meta[3])
        keep_ref[slot] = jnp.zeros(keep_ref.shape[1:], BF16)
        send_ref[slot] = jnp.zeros(keep_ref.shape[1:], BF16)
        for index, part in enumerate((a, b, c, d)):
            @pl.when(jnp.logical_and(mine, step == index))
            def _(part=part):
                keep_ref[slot] = part[half, :, keep_at]
                send_ref[slot] = part[half, :, send_at]


def chosen_weight(meta, parts):
    width = parts[0].shape[2] // 2
    return pl.pallas_call(
        choose_weight_kernel,
        out_shape=[shape((NB, 32, width), BF16)] * 2,
        in_specs=[SMEM] + whole(CHIPS),
        out_specs=whole(2),
        compiler_params=params(),
        cost_estimate=cost(10**6, 2 * 10**6),
    )(meta, *parts)


def update_kernel(meta, *refs):
    gains, kept_parts = refs[:2], refs[2:2 + CHIPS]
    own_ref, other_ref, out_ref, gain, kept = refs[2 + CHIPS:]
    core = meta[3]
    for group in range(2):
        place = core if group == 0 else 1 - core
        gain[pl.ds(pl.multiple_of(place * 256, 256), 256), :] = gains[group][...]
    for step in range(CHIPS):
        row = behind(meta[2], step)
        for slot in range(NB):
            start = pl.multiple_of(slot * BLOCK + row * 32, 32)
            kept[pl.ds(start, 32), :] = kept_parts[step][slot]
    width = out_ref.shape[1]
    keeps = []
    for place in range(2):
        for half in range(2):
            number = ((meta[1] * CHIPS + meta[2]) * 2 + place) * 2 + half
            keep = jnp.float32(1.0)
            for slot in range(NB):
                keep = jnp.where(block_number(meta, slot) == number, 0.0, keep)
            keeps.append(keep)
    for col in range(0, width, 256):
        update = jnp.dot(gain[...], kept[:, col:col + 256], preferred_element_type=F32)
        for group in range(4):
            rows = slice(group * BLOCK, (group + 1) * BLOCK)
            local = slice((group % 2) * BLOCK, (group % 2 + 1) * BLOCK)
            mine = own_ref[local, col:col + 256].astype(F32)
            other = other_ref[local, col:col + 256].astype(F32)
            before = jnp.where(core == group // 2, mine, other)
            out_ref[rows, col:col + 256] = ((before - update[rows]) * keeps[group]).astype(BF16)


def updated(meta, gains, kept_parts, own, other):
    width = own.shape[1]
    return pl.pallas_call(
        update_kernel,
        out_shape=shape((512, width), BF16),
        in_specs=[SMEM] + whole(CHIPS + 4),
        out_specs=pl.BlockSpec(memory_space=pltpu.VMEM),
        scratch_shapes=[pltpu.VMEM((512, N), BF16), pltpu.VMEM((N, width), BF16)],
        compiler_params=params(),
        cost_estimate=cost(10**9, 6 * 10**6),
    )(meta, *gains, *kept_parts, own, other)


def project_kernel(meta, tokens_ref, own_ref, other_ref, out_ref):
    width = own_ref.shape[1]
    core = meta[3]
    own_at = pl.ds(pl.multiple_of(core * width, BLOCK), width)
    other_at = pl.ds(pl.multiple_of((1 - core) * width, BLOCK), width)
    out_ref[...] = (
        lax.dot_general(own_ref[...], tokens_ref[:, own_at], (((1,), (1,)), ((), ())),
                        preferred_element_type=F32)
        + lax.dot_general(other_ref[...], tokens_ref[:, other_at], (((1,), (1,)), ((), ())),
                          preferred_element_type=F32)
    ).astype(out_ref.dtype)


def projected(meta, tokens, own, other, step, dtype):
    count, width = tokens.shape[0] // CHIPS, tokens.shape[1]
    full = pl.BlockSpec(own.shape, lambda i, meta: (0, 0))
    return pl.pallas_call(
        project_kernel,
        out_shape=shape((own.shape[0], count), dtype),
        grid_spec=pltpu.PrefetchScalarGridSpec(
            num_scalar_prefetch=1,
            grid=(1,),
            in_specs=[
                pl.BlockSpec((count, width), lambda i, meta: (ahead(meta[0], step), 0)),
                full,
                full,
            ],
            out_specs=pl.BlockSpec((own.shape[0], count), lambda i, meta: (0, 0)),
        ),
        compiler_params=params(),
        cost_estimate=cost(10**9, 4 * 10**6),
    )(meta, tokens, own, other)


def gram_kernel(mirror, meta, *refs):
    own, first, second = refs[:CHIPS], refs[CHIPS:2 * CHIPS], refs[2 * CHIPS:3 * CHIPS]
    out_ref, left = refs[3 * CHIPS:]
    x, y, z, core = meta[0], meta[1], meta[2], meta[3]
    rows = pl.ds(pl.multiple_of((1 - core if mirror else core) * 256, 256), 256)
    for step in range(CHIPS):
        at = lax.rem(y - x + step + CHIPS, CHIPS)
        left[:, pl.ds(pl.multiple_of(at * BLOCK, BLOCK), BLOCK)] = own[step][rows, :BLOCK]
        left[:, pl.ds(pl.multiple_of((at + CHIPS) * BLOCK, BLOCK), BLOCK)] = own[step][rows, BLOCK:]
    width = first[0].shape[1]
    for step in range(CHIPS):
        right = jnp.concatenate(
            [first[back][step] for back in range(CHIPS)]
            + [second[step][back] for back in range(CHIPS)], axis=1)
        at = pl.multiple_of(behind(z, step) * width, width)
        out_ref[:, pl.ds(at, width)] = lax.dot_general(
            left[...], right, (((1,), (1,)), ((), ())), preferred_element_type=F32
        ).astype(out_ref.dtype)


def gram_rows(meta, own, first, second, mirror, dtype):
    rows, width = 256, first[0].shape[1] * CHIPS
    return pl.pallas_call(
        lambda *refs: gram_kernel(mirror, *refs),
        out_shape=shape((rows, width), dtype),
        in_specs=[SMEM] + whole(3 * CHIPS),
        out_specs=pl.BlockSpec(memory_space=pltpu.VMEM),
        scratch_shapes=[pltpu.VMEM((rows, 2 * CHIPS * BLOCK), BF16)],
        compiler_params=params(),
        cost_estimate=cost(2 * 10**9, 6 * 10**6),
    )(meta, *own, *first, *second)


def device_id(x, y, z, c):
    return ((y * CHIPS + z) * 2 + c) * CHIPS + x


def permute(value, target):
    pairs = []
    for x in range(CHIPS):
        for y in range(CHIPS):
            for z in range(CHIPS):
                for c in range(2):
                    pairs.append((device_id(x, y, z, c), device_id(*target(x, y, z, c))))
    return lax.ppermute(value, AXES, pairs)


def shifted(value, axis, step):
    def target(x, y, z, c):
        at = [x, y, z, c]
        at[axis] = (at[axis] + step) % CHIPS
        return at

    return permute(value, target)


def partner(value):
    return permute(value, lambda x, y, z, c: (x, y, z, 1 - c))


def gathered(value, axis):
    far, near, back = (shifted(value, axis, step) for step in (2, 1, 3))
    return [value, near, far, back]


def exchanged(parts, axis):
    far, near, back = (shifted(parts[step], axis, step) for step in (2, 1, 3))
    return [parts[0], near, far, back]


def after(value, *others):
    return lax.optimization_barrier((value,) + others)[0]


def shards(calib, weight, inverse_factor, pruned_blocks):
    rows_dev, width_dev = weight.shape
    full_width = width_dev * CHIPS
    r = lax.axis_index("rows")
    x = lax.axis_index("mp")
    core = lax.rem(r, 2)
    meta = jnp.concatenate(
        [jnp.stack([x, lax.div(r, 8), lax.rem(lax.div(r, 2), CHIPS), core]), pruned_blocks]
    ).astype(jnp.int32)
    token_count = calib.shape[0] * 32

    columns, keep, send = turned_rows(meta, exchanged(pruned_columns(meta, inverse_factor), 0))
    line_part = jnp.stack([keep, partner(send)])

    *cut, own_weight, send_weight = weight_rows(meta, weight)
    other_weight = partner(send_weight)
    keep, send = chosen_weight(after(meta, line_part), exchanged(cut, 2))
    columns = gathered(columns, 0)
    line = gathered(line_part, 2)
    kept_line = after(keep, *line) + partner(send)

    parts = gathered(chosen_rows(after(meta, kept_line), line), 1)
    kept_sums = gathered(kept_line, 1)
    kept_quarter = (kept_sums[0] + kept_sums[1]) + (kept_sums[2] + kept_sums[3])
    parts[0] = after(parts[0], kept_quarter, *columns)
    total = (parts[0] + parts[1]) + (parts[2] + parts[3])
    kept_parts = gathered(kept_quarter, 2)
    pieces = []
    for piece in gathered(total, 0):
        pieces += [piece, partner(piece)]

    plane = [[core_at + 2 * chip for chip in range(16)] for core_at in range(2)]
    calib = after(calib, total, *kept_parts)
    tokens = lax.all_gather(calib, "rows", axis=0, tiled=True, axis_index_groups=plane)

    gain = solve(after(meta, *kept_parts), pieces, columns)
    gains = [gain, partner(gain)]
    pruned = updated(meta, gains, kept_parts, own_weight, other_weight)
    pruned_other = partner(pruned)
    mine = lax.dynamic_slice_in_dim(pruned, core * rows_dev, rows_dev, 0)
    theirs = lax.dynamic_slice_in_dim(pruned_other, core * rows_dev, rows_dev, 0)
    pruned_weight = jnp.where(
        core == 0, jnp.concatenate([mine, theirs], axis=1), jnp.concatenate([theirs, mine], axis=1)
    )

    sends = {step: projected(meta, tokens, pruned, pruned_other, step, BF16) for step in (2, 1, 3)}
    got = [shifted(sends[step], 0, step) for step in (2, 1, 3)]
    summed = projected(meta, tokens, pruned, pruned_other, 0, F32)
    for value in got:
        summed = summed + value.astype(F32)
    chunk = (summed * float(full_width) ** (-0.5)).astype(BF16)

    crossed = [
        permute(part, lambda x, y, z, c: (y, x, z, c)) for part in (chunk[:, :BLOCK], chunk[:, BLOCK:])
    ]
    by_z = jnp.stack(gathered(crossed[0], 2))
    by_y = jnp.stack(gathered(crossed[1], 1))
    first = gathered(by_z, 1)
    second = gathered(by_y, 2)
    own = gathered(after(chunk, *crossed), 0)
    given = partner(gram_rows(after(meta, pruned_weight), own, first, second, True, BF16))
    gram_block = (gram_rows(meta, own, first, second, False, F32) + given.astype(F32)) / token_count
    return (pruned_weight, gram_block)


def solution(mesh):
    return jax.shard_map(
        shards,
        mesh=mesh,
        in_specs=(P("rows", "mp"), P("rows", "mp"), P("rows", "mp"), P()),
        out_specs=(P("rows", "mp"), P("rows", "mp")),
        check_vma=False,
    )
```

```python
import jax
import jax.numpy as jnp
from jax import lax
from jax.experimental import pallas as pl
from jax.experimental.pallas import tpu as pltpu
from jax.sharding import PartitionSpec as P

BLOCK = 128
NB = 7
F32 = jnp.float32
GROUPS = BLOCK // 8
PANEL = 4


def dot_full(a, b):
    return lax.dot_general(
        a, b, (((1,), (0,)), ((), ())), precision=lax.Precision.HIGHEST, preferred_element_type=F32
    )


def dot_once(a, b):
    return lax.dot_general(a, b, (((1,), (0,)), ((), ())), preferred_element_type=F32)


def halves(a):
    high = a.astype(jnp.bfloat16)
    return high, (a - high.astype(F32)).astype(jnp.bfloat16)


def dot_split(a, b):
    (a_high, a_low), (b_high, b_low) = halves(a), halves(b)
    return dot_once(a_high, b_high) + (dot_once(a_high, b_low) + dot_once(a_low, b_high))


def spread(v):
    return jnp.broadcast_to(v, (8, BLOCK))


def lane_of(v, k):
    return jnp.take_along_axis(v, jnp.full((8, BLOCK), k, jnp.int32), axis=1)


def tree(terms):
    while len(terms) > 1:
        terms = [
            terms[i] + terms[i + 1] if i + 1 < len(terms) else terms[i]
            for i in range(0, len(terms), 2)
        ]
    return terms[0]


def invert_small(e):
    n = len(e)
    if n == 2:
        a, b, d = e[0][0], e[0][1], e[1][1]
        r = 1.0 / (a * d - b * b)
        off = -(b * r)
        return [[d * r, off], [off, a * r]]
    h = n // 2
    p = invert_small([row[:h] for row in e[:h]])
    b = [row[h:] for row in e[:h]]
    w = [[tree([p[i][k] * b[k][j] for k in range(h)]) for j in range(h)] for i in range(h)]
    s = [[None] * h for _ in range(h)]
    for i in range(h):
        for j in range(i, h):
            s[i][j] = s[j][i] = e[h + i][h + j] - tree([b[k][i] * w[k][j] for k in range(h)])
    t = invert_small(s)
    v = [[tree([w[i][k] * t[k][j] for k in range(h)]) for j in range(h)] for i in range(h)]
    q = [[None] * n for _ in range(n)]
    for i in range(h):
        for j in range(h):
            q[h + i][h + j] = t[i][j]
            q[i][h + j] = q[h + j][i] = -v[i][j]
        for j in range(i, h):
            q[i][j] = q[j][i] = p[i][j] + tree([v[i][k] * w[j][k] for k in range(h)])
    return q


def panel_steps(groups, first, lane, sub):
    for home in range(len(groups)):
        k = first + 8 * home
        cols = [[lane_of(group, k + t) for t in range(8)] for group in groups]
        e = [[None] * 8 for _ in range(8)]
        for t in range(8):
            for s in range(t + 1):
                e[s][t] = e[t][s] = spread(cols[home][t][s:s + 1, :])
        q = invert_small(e)
        inside = (lane >= k) & (lane < k + 8)
        rows = [
            jnp.where(lane == k + t, 1.0, jnp.where(inside, 0.0, spread(groups[home][t:t + 1, :])))
            for t in range(8)
        ]
        new = [tree([q[t][i] * rows[i] for i in range(8)]) for t in range(8)]
        out = []
        for g, group in enumerate(groups):
            if g == home:
                v = new[0]
                for t in range(1, 8):
                    v = jnp.where(sub == t, new[t], v)
            else:
                v = jnp.where(inside, 0.0, group) - tree([cols[g][t] * new[t] for t in range(8)])
            out.append(v)
        groups = out
    return groups


def invert_block(groups, lane, sub):
    for first in range(0, GROUPS, PANEL):
        panel = panel_steps(groups[first:first + PANEL], first * 8, lane, sub)
        inside = (lane >= first * 8) & (lane < (first + PANEL) * 8)
        left = jnp.concatenate(groups, axis=0)[:, first * 8:(first + PANEL) * 8]
        change = dot_full(left, jnp.concatenate(panel, axis=0))
        groups = [
            panel[g - first]
            if first <= g < first + PANEL
            else jnp.where(inside, 0.0, groups[g]) - change[g * 8:g * 8 + 8, :]
            for g in range(GROUPS)
        ]
    return groups


CHIPS = 4
TURNS = NB // 2 + 1
AXES = ("rows", "mp")
N = NB * BLOCK
BF16 = jnp.bfloat16
META = 4
CUT = 4


def whole(count):
    return [pl.BlockSpec(memory_space=pltpu.VMEM)] * count


SMEM = pl.BlockSpec(memory_space=pltpu.SMEM)
ANY = pl.BlockSpec(memory_space=pl.ANY)


def cost(flops, data):
    return pl.CostEstimate(flops=flops, bytes_accessed=data, transcendentals=0)


def params():
    return pltpu.CompilerParams(vmem_limit_bytes=44 * 2**20)


def shape(dims, dtype):
    return jax.ShapeDtypeStruct(dims, dtype)


def ahead(place, step):
    return lax.rem(place + step, CHIPS)


def behind(place, step):
    return lax.rem(place - step + CHIPS, CHIPS)


def block_number(meta, slot):
    return meta[META + slot]


def columns_kernel(meta, source, *refs):
    outs, buffer, sems = refs[:CHIPS], refs[CHIPS], refs[CHIPS + 1]
    width = source.shape[1]
    inside = []
    for slot in range(NB):
        offset = block_number(meta, slot) * BLOCK - meta[0] * width
        ok = jnp.logical_and(offset >= 0, offset < width)
        inside.append(jnp.where(ok, 1.0, 0.0).astype(F32))
        start = pl.multiple_of(jnp.clip(offset, 0, width - BLOCK), BLOCK)
        pltpu.make_async_copy(source.at[:, pl.ds(start, BLOCK)], buffer.at[slot], sems.at[slot]).start()
    for slot in range(NB):
        pltpu.make_async_copy(source.at[:, pl.ds(0, BLOCK)], buffer.at[slot], sems.at[slot]).wait()
        for step in range(CHIPS):
            quarter = ahead(meta[0], step)
            for half in range(2):
                start = pl.multiple_of(half * BLOCK + quarter * 32, 32)
                outs[step][half, :, slot * BLOCK:(slot + 1) * BLOCK] = (
                    buffer[slot, pl.ds(start, 32), :] * inside[slot]
                )


def pruned_columns(meta, inverse_factor):
    return pl.pallas_call(
        columns_kernel,
        out_shape=[shape((2, 32, N), F32)] * CHIPS,
        in_specs=[SMEM, ANY],
        out_specs=whole(CHIPS),
        scratch_shapes=[
            pltpu.VMEM((NB, inverse_factor.shape[0], BLOCK), F32),
            pltpu.SemaphoreType.DMA((NB,)),
        ],
        compiler_params=params(),
        cost_estimate=cost(10**6, 6 * 10**6),
    )(meta, inverse_factor)


def turn_kernel(meta, a, b, c, d, columns_ref, keep_ref, send_ref, doubled):
    core = meta[3]
    number = (meta[1] * CHIPS + meta[2]) * 2 + core
    for half in range(2):
        total = (a[half] + b[half]) + (c[half] + d[half])
        columns_ref[half * 32:(half + 1) * 32, :] = total
        doubled[half * 32:(half + 1) * 32, :N] = total
        doubled[half * 32:(half + 1) * 32, N:] = total[:, :(TURNS - 1) * BLOCK]
    for half in range(2):
        slot = jnp.int32(0)
        for candidate in range(NB):
            slot = jnp.where(block_number(meta, candidate) == 2 * number + half, candidate, slot)
        lanes = pl.ds(pl.multiple_of(slot * BLOCK, BLOCK), TURNS * BLOCK)
        keep_ref[half] = doubled[pl.ds(pl.multiple_of(half * 32 + core * 16, 16), 16), lanes]
        send_ref[half] = doubled[pl.ds(pl.multiple_of(half * 32 + (1 - core) * 16, 16), 16), lanes]


def turned_rows(meta, parts):
    return pl.pallas_call(
        turn_kernel,
        out_shape=[shape((64, N), F32)] + [shape((2, 16, TURNS * BLOCK), F32)] * 2,
        in_specs=[SMEM] + whole(CHIPS),
        out_specs=whole(3),
        scratch_shapes=[pltpu.VMEM((64, N + (TURNS - 1) * BLOCK), F32)],
        compiler_params=params(),
        cost_estimate=cost(10**6, 2 * 10**6),
    )(meta, *parts)


def source_of(meta, slot):
    block = block_number(meta, slot)
    y, z = lax.div(block, 16), lax.rem(lax.div(block, 4), 4)
    return y, behind(meta[2], z), lax.rem(lax.div(block, 2), 2), lax.rem(block, 2)


def choose_kernel(meta, a, b, c, d, out_ref):
    for slot in range(NB):
        y, step, core, half = source_of(meta, slot)
        apart = jnp.where(core == meta[3], 0, 1)
        out_ref[slot] = jnp.zeros(out_ref.shape[1:], out_ref.dtype)
        for index, part in enumerate((a, b, c, d)):
            @pl.when(jnp.logical_and(y == meta[1], step == index))
            def _(part=part):
                out_ref[slot] = part[apart, half]


def chosen_rows(meta, parts):
    return pl.pallas_call(
        choose_kernel,
        out_shape=shape((NB, 16, TURNS * BLOCK), F32),
        in_specs=[SMEM] + whole(CHIPS),
        out_specs=pl.BlockSpec(memory_space=pltpu.VMEM),
        compiler_params=params(),
        cost_estimate=cost(10**6, 10**6),
    )(meta, *parts)


def eliminate(work, numbers, lane, sub):
    for k in numbers:
        lo, hi = k * BLOCK, (k + 1) * BLOCK
        groups = invert_block([work[lo + g * 8:lo + g * 8 + 8, lo:hi] for g in range(GROUPS)], lane, sub)
        pivot = jnp.concatenate(groups, axis=0)
        if k + 1 < NB:
            upper = work[lo:hi, hi:]
            lower = dot_full(work[hi:N, lo:hi], pivot)
            work[hi:N, hi:] -= dot_full(lower, upper)
            work[hi:N, lo:hi] = lower
        gain = dot_split(work[N:, lo:hi], pivot)
        if k + 1 < NB:
            work[N:, hi:] -= dot_split(gain, upper)
        work[N:, lo:hi] = gain


def first_kernel(meta, *refs):
    pieces, columns = refs[:2 * CHIPS], refs[2 * CHIPS:3 * CHIPS]
    work = refs[3 * CHIPS]
    for step in range(CHIPS):
        quarter = behind(meta[0], step)
        for other in range(2):
            place = quarter * 32 + (meta[3] if other == 0 else 1 - meta[3]) * 16
            for slot in range(NB):
                start = pl.multiple_of(slot * BLOCK + place, 16)
                for turn in range(TURNS):
                    col = (slot + turn) % NB
                    work[pl.ds(start, 16), col * BLOCK:(col + 1) * BLOCK] = pieces[2 * step + other][
                        slot, :, turn * BLOCK:(turn + 1) * BLOCK]
        for half in range(2):
            start = pl.multiple_of(N + half * BLOCK + quarter * 32, 32)
            work[pl.ds(start, 32), :] = columns[step][half * 32:(half + 1) * 32, :]
    for slot in range(NB):
        for turn in range(1, TURNS):
            col = (slot + turn) % NB
            work[col * BLOCK:(col + 1) * BLOCK, slot * BLOCK:(slot + 1) * BLOCK] = work[
                slot * BLOCK:(slot + 1) * BLOCK, col * BLOCK:(col + 1) * BLOCK].T
    lane = lax.broadcasted_iota(jnp.int32, (8, BLOCK), 1)
    sub = lax.broadcasted_iota(jnp.int32, (8, BLOCK), 0)
    eliminate(work, range(CUT), lane, sub)


def second_kernel(meta, begun, gain_ref, work):
    work[...] = begun[...]
    lane = lax.broadcasted_iota(jnp.int32, (8, BLOCK), 1)
    sub = lax.broadcasted_iota(jnp.int32, (8, BLOCK), 0)
    eliminate(work, range(CUT, NB), lane, sub)
    gain_ref[:, N - BLOCK:] = work[N:, N - BLOCK:].astype(gain_ref.dtype)
    for k in range(NB - 2, -1, -1):
        lo, hi = k * BLOCK, (k + 1) * BLOCK
        work[N:, lo:hi] -= dot_split(work[N:, hi:], work[hi:N, lo:hi])
        gain_ref[:, lo:hi] = work[N:, lo:hi].astype(gain_ref.dtype)


def solve_first(meta, pieces, columns):
    extra = CHIPS * columns[0].shape[0]
    return pl.pallas_call(
        first_kernel,
        out_shape=shape((N + extra, N), F32),
        in_specs=[SMEM] + whole(3 * CHIPS),
        out_specs=pl.BlockSpec(memory_space=pltpu.VMEM),
        compiler_params=params(),
        cost_estimate=cost(3 * 10**10, 10**7),
    )(meta, *pieces, *columns)


def solve_second(meta, begun):
    return pl.pallas_call(
        second_kernel,
        out_shape=shape((begun.shape[0] - N, N), BF16),
        in_specs=[SMEM] + whole(1),
        out_specs=pl.BlockSpec(memory_space=pltpu.VMEM),
        scratch_shapes=[pltpu.VMEM(begun.shape, F32)],
        compiler_params=params(),
        cost_estimate=cost(3 * 10**10, 10**7),
    )(meta, begun)


def rows_kernel(meta, weight_ref, *refs):
    outs, keep_ref, send_ref = refs[:CHIPS], refs[CHIPS], refs[CHIPS + 1]
    width = weight_ref.shape[1] // 2
    for step in range(CHIPS):
        quarter = ahead(meta[2], step)
        for half in range(2):
            start = pl.multiple_of(half * BLOCK + quarter * 32, 32)
            outs[step][half] = weight_ref[pl.ds(start, 32), :]
    keep_ref[...] = weight_ref[:, pl.ds(pl.multiple_of(meta[3] * width, BLOCK), width)]
    send_ref[...] = weight_ref[:, pl.ds(pl.multiple_of((1 - meta[3]) * width, BLOCK), width)]


def weight_rows(meta, weight):
    rows, width = weight.shape
    return pl.pallas_call(
        rows_kernel,
        out_shape=[shape((2, 32, width), BF16)] * CHIPS + [shape((rows, width // 2), BF16)] * 2,
        in_specs=[SMEM] + whole(1),
        out_specs=whole(CHIPS + 2),
        compiler_params=params(),
        cost_estimate=cost(10**6, 4 * 10**6),
    )(meta, weight)


def choose_weight_kernel(meta, a, b, c, d, keep_ref, send_ref):
    width = keep_ref.shape[2]
    keep_at = pl.ds(pl.multiple_of(meta[3] * width, BLOCK), width)
    send_at = pl.ds(pl.multiple_of((1 - meta[3]) * width, BLOCK), width)
    for slot in range(NB):
        y, step, core, half = source_of(meta, slot)
        mine = jnp.logical_and(y == meta[1], core == meta[3])
        keep_ref[slot] = jnp.zeros(keep_ref.shape[1:], BF16)
        send_ref[slot] = jnp.zeros(keep_ref.shape[1:], BF16)
        for index, part in enumerate((a, b, c, d)):
            @pl.when(jnp.logical_and(mine, step == index))
            def _(part=part):
                keep_ref[slot] = part[half, :, keep_at]
                send_ref[slot] = part[half, :, send_at]


def chosen_weight(meta, parts):
    width = parts[0].shape[2] // 2
    return pl.pallas_call(
        choose_weight_kernel,
        out_shape=[shape((NB, 32, width), BF16)] * 2,
        in_specs=[SMEM] + whole(CHIPS),
        out_specs=whole(2),
        compiler_params=params(),
        cost_estimate=cost(10**6, 2 * 10**6),
    )(meta, *parts)


def update_rows(meta, place, gain_ref, kept, before_ref, out_ref):
    keeps = []
    for half in range(2):
        number = ((meta[1] * CHIPS + meta[2]) * 2 + place) * 2 + half
        keep = jnp.float32(1.0)
        for slot in range(NB):
            keep = jnp.where(block_number(meta, slot) == number, 0.0, keep)
        keeps.append(keep)
    for col in range(0, out_ref.shape[1], 256):
        update = jnp.dot(gain_ref[...], kept[:, col:col + 256], preferred_element_type=F32)
        for half in range(2):
            rows = slice(half * BLOCK, (half + 1) * BLOCK)
            before = before_ref[rows, col:col + 256].astype(F32)
            out_ref[rows, col:col + 256] = ((before - update[rows]) * keeps[half]).astype(BF16)


def own_update_kernel(meta, gain_ref, *refs):
    parts, (before_ref, out_ref, kept) = refs[:CHIPS], refs[CHIPS:]
    for step in range(CHIPS):
        row = behind(meta[2], step)
        for slot in range(NB):
            start = pl.multiple_of(slot * BLOCK + row * 32, 32)
            kept[pl.ds(start, 32), :] = parts[step][slot]
    update_rows(meta, meta[3], gain_ref, kept, before_ref, out_ref)


def other_update_kernel(meta, gain_ref, kept, before_ref, out_ref):
    update_rows(meta, 1 - meta[3], gain_ref, kept, before_ref, out_ref)


def updated_own(meta, gain, kept_parts, before):
    return pl.pallas_call(
        own_update_kernel,
        out_shape=[shape(before.shape, BF16), shape((N, before.shape[1]), BF16)],
        in_specs=[SMEM] + whole(CHIPS + 2),
        out_specs=whole(2),
        compiler_params=params(),
        cost_estimate=cost(10**9, 6 * 10**6),
    )(meta, gain, *kept_parts, before)


def updated_other(meta, gain, kept, before):
    return pl.pallas_call(
        other_update_kernel,
        out_shape=shape(before.shape, BF16),
        in_specs=[SMEM] + whole(3),
        out_specs=pl.BlockSpec(memory_space=pltpu.VMEM),
        compiler_params=params(),
        cost_estimate=cost(10**9, 4 * 10**6),
    )(meta, gain, kept, before)


def dot_last(a, b):
    return lax.dot_general(a, b, (((1,), (1,)), ((), ())), preferred_element_type=F32)


def project_kernel(meta, tokens_ref, own_left, own_right, other_left, other_right, out_ref):
    rows, width = own_left.shape
    core = meta[3]
    left = tokens_ref[:, pl.ds(pl.multiple_of(core * width, BLOCK), width)]
    right = tokens_ref[:, pl.ds(pl.multiple_of((1 - core) * width, BLOCK), width)]
    own_at = pl.ds(pl.multiple_of(core * rows, rows), rows)
    other_at = pl.ds(pl.multiple_of((1 - core) * rows, rows), rows)
    out_ref[own_at, :] = (
        dot_last(own_left[...], left) + dot_last(own_right[...], right)
    ).astype(out_ref.dtype)
    out_ref[other_at, :] = (
        dot_last(other_left[...], left) + dot_last(other_right[...], right)
    ).astype(out_ref.dtype)


def projected(meta, tokens, parts, step, dtype):
    count, width = tokens.shape[0] // CHIPS, tokens.shape[1]
    rows = parts[0].shape[0]
    full = pl.BlockSpec(parts[0].shape, lambda i, meta: (0, 0))
    return pl.pallas_call(
        project_kernel,
        out_shape=shape((2 * rows, count), dtype),
        grid_spec=pltpu.PrefetchScalarGridSpec(
            num_scalar_prefetch=1,
            grid=(1,),
            in_specs=[pl.BlockSpec((count, width), lambda i, meta: (ahead(meta[0], step), 0))]
            + [full] * 4,
            out_specs=pl.BlockSpec((2 * rows, count), lambda i, meta: (0, 0)),
        ),
        compiler_params=params(),
        cost_estimate=cost(10**9, 4 * 10**6),
    )(meta, tokens, *parts)


def gram_kernel(mirror, meta, *refs):
    own, first, second = refs[:CHIPS], refs[CHIPS:2 * CHIPS], refs[2 * CHIPS:3 * CHIPS]
    out_ref, left = refs[3 * CHIPS:]
    x, y, z, core = meta[0], meta[1], meta[2], meta[3]
    rows = pl.ds(pl.multiple_of((1 - core if mirror else core) * 256, 256), 256)
    for step in range(CHIPS):
        at = lax.rem(y - x + step + CHIPS, CHIPS)
        left[:, pl.ds(pl.multiple_of(at * BLOCK, BLOCK), BLOCK)] = own[step][rows, :BLOCK]
        left[:, pl.ds(pl.multiple_of((at + CHIPS) * BLOCK, BLOCK), BLOCK)] = own[step][rows, BLOCK:]
    width = first[0].shape[1]
    for step in range(CHIPS):
        right = jnp.concatenate(
            [first[back][step] for back in range(CHIPS)]
            + [second[step][back] for back in range(CHIPS)], axis=1)
        at = pl.multiple_of(behind(z, step) * width, width)
        out_ref[:, pl.ds(at, width)] = lax.dot_general(
            left[...], right, (((1,), (1,)), ((), ())), preferred_element_type=F32
        ).astype(out_ref.dtype)


def gram_rows(meta, own, first, second, mirror, dtype):
    rows, width = 256, first[0].shape[1] * CHIPS
    return pl.pallas_call(
        lambda *refs: gram_kernel(mirror, *refs),
        out_shape=shape((rows, width), dtype),
        in_specs=[SMEM] + whole(3 * CHIPS),
        out_specs=pl.BlockSpec(memory_space=pltpu.VMEM),
        scratch_shapes=[pltpu.VMEM((rows, 2 * CHIPS * BLOCK), BF16)],
        compiler_params=params(),
        cost_estimate=cost(2 * 10**9, 6 * 10**6),
    )(meta, *own, *first, *second)


def device_id(x, y, z, c):
    return ((y * CHIPS + z) * 2 + c) * CHIPS + x


def permute(value, target):
    pairs = []
    for x in range(CHIPS):
        for y in range(CHIPS):
            for z in range(CHIPS):
                for c in range(2):
                    pairs.append((device_id(x, y, z, c), device_id(*target(x, y, z, c))))
    return lax.ppermute(value, AXES, pairs)


def shifted(value, axis, step):
    def target(x, y, z, c):
        at = [x, y, z, c]
        at[axis] = (at[axis] + step) % CHIPS
        return at

    return permute(value, target)


def partner(value):
    return permute(value, lambda x, y, z, c: (x, y, z, 1 - c))


def gathered(value, axis):
    far, near, back = (shifted(value, axis, step) for step in (2, 1, 3))
    return [value, near, far, back]


def exchanged(parts, axis):
    far, near, back = (shifted(parts[step], axis, step) for step in (2, 1, 3))
    return [parts[0], near, far, back]


def after(value, *others):
    return lax.optimization_barrier((value,) + others)[0]


def shards(calib, weight, inverse_factor, pruned_blocks):
    rows_dev, width_dev = weight.shape
    full_width = width_dev * CHIPS
    r = lax.axis_index("rows")
    x = lax.axis_index("mp")
    core = lax.rem(r, 2)
    meta = jnp.concatenate(
        [jnp.stack([x, lax.div(r, 8), lax.rem(lax.div(r, 2), CHIPS), core]), pruned_blocks]
    ).astype(jnp.int32)
    token_count = calib.shape[0] * 32

    plane = [[core_at + 2 * chip for chip in range(16)] for core_at in range(2)]
    tokens = lax.all_gather(calib, "rows", axis=0, tiled=True, axis_index_groups=plane)

    columns, keep, send = turned_rows(meta, exchanged(pruned_columns(meta, inverse_factor), 0))
    line = gathered(jnp.stack([keep, partner(send)]), 2)
    columns = gathered(columns, 0)
    parts = gathered(chosen_rows(meta, line), 1)
    parts[0] = after(parts[0], *columns)
    total = (parts[0] + parts[1]) + (parts[2] + parts[3])
    pieces = []
    for piece in gathered(total, 0):
        pieces += [piece, partner(piece)]

    *cut, own_weight, send_weight = weight_rows(meta, weight)
    other_weight = partner(send_weight)
    keep, send = chosen_weight(after(meta, pieces[2]), exchanged(cut, 2))
    kept_line = keep + partner(send)
    begun = solve_first(after(meta, kept_line), pieces, columns)
    kept_sums = gathered(kept_line, 1)
    kept_quarter = (kept_sums[0] + kept_sums[1]) + (kept_sums[2] + kept_sums[3])
    gain = solve_second(after(meta, kept_quarter), begun)
    kept_parts = gathered(kept_quarter, 2)

    own_left, kept = updated_own(meta, gain, kept_parts, own_weight)
    other_left = updated_other(meta, partner(gain), kept, other_weight)
    other_right, own_right = partner(own_left), partner(other_left)
    pruned_weight = jnp.where(
        core == 0,
        jnp.concatenate([own_left, own_right], axis=1),
        jnp.concatenate([own_right, own_left], axis=1),
    )

    sides = [own_left, own_right, other_left, other_right]
    sends = {step: projected(meta, tokens, sides, step, BF16) for step in (2, 1, 3)}
    got = [shifted(sends[step], 0, step) for step in (2, 1, 3)]
    summed = projected(meta, tokens, sides, 0, F32)
    for value in got:
        summed = summed + value.astype(F32)
    chunk = (summed * float(full_width) ** (-0.5)).astype(BF16)

    crossed = [
        permute(part, lambda x, y, z, c: (y, x, z, c)) for part in (chunk[:, :BLOCK], chunk[:, BLOCK:])
    ]
    crossed = lax.optimization_barrier(tuple(crossed))
    by_z = jnp.stack(gathered(crossed[0], 2))
    by_y = jnp.stack(gathered(crossed[1], 1))
    first = gathered(by_z, 1)
    second = gathered(by_y, 2)
    own = gathered(after(chunk, *crossed), 0)
    given = partner(gram_rows(after(meta, pruned_weight), own, first, second, True, BF16))
    gram_block = (gram_rows(meta, own, first, second, False, F32) + given.astype(F32)) / token_count
    return (pruned_weight, gram_block)


def solution(mesh):
    return jax.shard_map(
        shards,
        mesh=mesh,
        in_specs=(P("rows", "mp"), P("rows", "mp"), P("rows", "mp"), P()),
        out_specs=(P("rows", "mp"), P("rows", "mp")),
        check_vma=False,
    )
```

```python
import jax
import jax.numpy as jnp
from jax import lax
from jax.experimental import pallas as pl
from jax.experimental.pallas import tpu as pltpu
from jax.sharding import PartitionSpec as P

BLOCK = 128
NB = 7
F32 = jnp.float32
GROUPS = BLOCK // 8
PANEL = 4


def dot_full(a, b):
    return lax.dot_general(
        a, b, (((1,), (0,)), ((), ())), precision=lax.Precision.HIGHEST, preferred_element_type=F32
    )


def dot_once(a, b):
    return lax.dot_general(a, b, (((1,), (0,)), ((), ())), preferred_element_type=F32)


def halves(a):
    high = a.astype(jnp.bfloat16)
    return high, (a - high.astype(F32)).astype(jnp.bfloat16)


def dot_split(a, b):
    (a_high, a_low), (b_high, b_low) = halves(a), halves(b)
    return dot_once(a_high, b_high) + (dot_once(a_high, b_low) + dot_once(a_low, b_high))


def spread(v):
    return jnp.broadcast_to(v, (8, BLOCK))


def lane_of(v, k):
    return jnp.take_along_axis(v, jnp.full((8, BLOCK), k, jnp.int32), axis=1)


def tree(terms):
    while len(terms) > 1:
        terms = [
            terms[i] + terms[i + 1] if i + 1 < len(terms) else terms[i]
            for i in range(0, len(terms), 2)
        ]
    return terms[0]


def invert_small(e):
    n = len(e)
    if n == 2:
        a, b, d = e[0][0], e[0][1], e[1][1]
        r = 1.0 / (a * d - b * b)
        off = -(b * r)
        return [[d * r, off], [off, a * r]]
    h = n // 2
    p = invert_small([row[:h] for row in e[:h]])
    b = [row[h:] for row in e[:h]]
    w = [[tree([p[i][k] * b[k][j] for k in range(h)]) for j in range(h)] for i in range(h)]
    s = [[None] * h for _ in range(h)]
    for i in range(h):
        for j in range(i, h):
            s[i][j] = s[j][i] = e[h + i][h + j] - tree([b[k][i] * w[k][j] for k in range(h)])
    t = invert_small(s)
    v = [[tree([w[i][k] * t[k][j] for k in range(h)]) for j in range(h)] for i in range(h)]
    q = [[None] * n for _ in range(n)]
    for i in range(h):
        for j in range(h):
            q[h + i][h + j] = t[i][j]
            q[i][h + j] = q[h + j][i] = -v[i][j]
        for j in range(i, h):
            q[i][j] = q[j][i] = p[i][j] + tree([v[i][k] * w[j][k] for k in range(h)])
    return q


def panel_steps(groups, first, lane, sub):
    for home in range(len(groups)):
        k = first + 8 * home
        cols = [[lane_of(group, k + t) for t in range(8)] for group in groups]
        e = [[None] * 8 for _ in range(8)]
        for t in range(8):
            for s in range(t + 1):
                e[s][t] = e[t][s] = spread(cols[home][t][s:s + 1, :])
        q = invert_small(e)
        inside = (lane >= k) & (lane < k + 8)
        rows = [
            jnp.where(lane == k + t, 1.0, jnp.where(inside, 0.0, spread(groups[home][t:t + 1, :])))
            for t in range(8)
        ]
        new = [tree([q[t][i] * rows[i] for i in range(8)]) for t in range(8)]
        out = []
        for g, group in enumerate(groups):
            if g == home:
                v = new[0]
                for t in range(1, 8):
                    v = jnp.where(sub == t, new[t], v)
            else:
                v = jnp.where(inside, 0.0, group) - tree([cols[g][t] * new[t] for t in range(8)])
            out.append(v)
        groups = out
    return groups


def invert_block(groups, lane, sub):
    for first in range(0, GROUPS, PANEL):
        panel = panel_steps(groups[first:first + PANEL], first * 8, lane, sub)
        inside = (lane >= first * 8) & (lane < (first + PANEL) * 8)
        left = jnp.concatenate(groups, axis=0)[:, first * 8:(first + PANEL) * 8]
        change = dot_full(left, jnp.concatenate(panel, axis=0))
        groups = [
            panel[g - first]
            if first <= g < first + PANEL
            else jnp.where(inside, 0.0, groups[g]) - change[g * 8:g * 8 + 8, :]
            for g in range(GROUPS)
        ]
    return groups


CHIPS = 4
TURNS = NB // 2 + 1
AXES = ("rows", "mp")
N = NB * BLOCK
BF16 = jnp.bfloat16
META = 4
CUT = 4


def whole(count):
    return [pl.BlockSpec(memory_space=pltpu.VMEM)] * count


SMEM = pl.BlockSpec(memory_space=pltpu.SMEM)
ANY = pl.BlockSpec(memory_space=pl.ANY)


def cost(flops, data):
    return pl.CostEstimate(flops=flops, bytes_accessed=data, transcendentals=0)


def params(mebibytes=16):
    return pltpu.CompilerParams(vmem_limit_bytes=mebibytes * 2**20)


def shape(dims, dtype):
    return jax.ShapeDtypeStruct(dims, dtype)


def ahead(place, step):
    return lax.rem(place + step, CHIPS)


def behind(place, step):
    return lax.rem(place - step + CHIPS, CHIPS)


def block_number(meta, slot):
    return meta[META + slot]


def columns_kernel(meta, source, *refs):
    outs, buffer, sems = refs[:CHIPS], refs[CHIPS], refs[CHIPS + 1]
    width = source.shape[1]
    inside = []
    for slot in range(NB):
        offset = block_number(meta, slot) * BLOCK - meta[0] * width
        ok = jnp.logical_and(offset >= 0, offset < width)
        inside.append(jnp.where(ok, 1.0, 0.0).astype(F32))
        start = pl.multiple_of(jnp.clip(offset, 0, width - BLOCK), BLOCK)
        pltpu.make_async_copy(source.at[:, pl.ds(start, BLOCK)], buffer.at[slot], sems.at[slot]).start()
    for slot in range(NB):
        pltpu.make_async_copy(source.at[:, pl.ds(0, BLOCK)], buffer.at[slot], sems.at[slot]).wait()
        for step in range(CHIPS):
            quarter = ahead(meta[0], step)
            for half in range(2):
                start = pl.multiple_of(half * BLOCK + quarter * 32, 32)
                outs[step][half, :, slot * BLOCK:(slot + 1) * BLOCK] = (
                    buffer[slot, pl.ds(start, 32), :] * inside[slot]
                )


def pruned_columns(meta, inverse_factor):
    return pl.pallas_call(
        columns_kernel,
        out_shape=[shape((2, 32, N), F32)] * CHIPS,
        in_specs=[SMEM, ANY],
        out_specs=whole(CHIPS),
        scratch_shapes=[
            pltpu.VMEM((NB, inverse_factor.shape[0], BLOCK), F32),
            pltpu.SemaphoreType.DMA((NB,)),
        ],
        compiler_params=params(),
        cost_estimate=cost(10**6, 6 * 10**6),
    )(meta, inverse_factor)


def turn_kernel(meta, a, b, c, d, columns_ref, keep_ref, send_ref, doubled):
    core = meta[3]
    number = (meta[1] * CHIPS + meta[2]) * 2 + core
    for half in range(2):
        total = (a[half] + b[half]) + (c[half] + d[half])
        columns_ref[half * 32:(half + 1) * 32, :] = total
        doubled[half * 32:(half + 1) * 32, :N] = total
        doubled[half * 32:(half + 1) * 32, N:] = total[:, :(TURNS - 1) * BLOCK]
    for half in range(2):
        slot = jnp.int32(0)
        for candidate in range(NB):
            slot = jnp.where(block_number(meta, candidate) == 2 * number + half, candidate, slot)
        lanes = pl.ds(pl.multiple_of(slot * BLOCK, BLOCK), TURNS * BLOCK)
        keep_ref[half] = doubled[pl.ds(pl.multiple_of(half * 32 + core * 16, 16), 16), lanes]
        send_ref[half] = doubled[pl.ds(pl.multiple_of(half * 32 + (1 - core) * 16, 16), 16), lanes]


def turned_rows(meta, parts):
    return pl.pallas_call(
        turn_kernel,
        out_shape=[shape((64, N), F32)] + [shape((2, 16, TURNS * BLOCK), F32)] * 2,
        in_specs=[SMEM] + whole(CHIPS),
        out_specs=whole(3),
        scratch_shapes=[pltpu.VMEM((64, N + (TURNS - 1) * BLOCK), F32)],
        compiler_params=params(),
        cost_estimate=cost(10**6, 2 * 10**6),
    )(meta, *parts)


def source_of(meta, slot):
    block = block_number(meta, slot)
    y, z = lax.div(block, 16), lax.rem(lax.div(block, 4), 4)
    return y, behind(meta[2], z), lax.rem(lax.div(block, 2), 2), lax.rem(block, 2)


def choose_kernel(meta, a, b, c, d, out_ref):
    for slot in range(NB):
        y, step, core, half = source_of(meta, slot)
        apart = jnp.where(core == meta[3], 0, 1)
        out_ref[slot] = jnp.zeros(out_ref.shape[1:], out_ref.dtype)
        for index, part in enumerate((a, b, c, d)):
            @pl.when(jnp.logical_and(y == meta[1], step == index))
            def _(part=part):
                out_ref[slot] = part[apart, half]


def chosen_rows(meta, parts):
    return pl.pallas_call(
        choose_kernel,
        out_shape=shape((NB, 16, TURNS * BLOCK), F32),
        in_specs=[SMEM] + whole(CHIPS),
        out_specs=pl.BlockSpec(memory_space=pltpu.VMEM),
        compiler_params=params(),
        cost_estimate=cost(10**6, 10**6),
    )(meta, *parts)


def eliminate(work, numbers, lane, sub):
    for k in numbers:
        lo, hi = k * BLOCK, (k + 1) * BLOCK
        groups = invert_block([work[lo + g * 8:lo + g * 8 + 8, lo:hi] for g in range(GROUPS)], lane, sub)
        pivot = jnp.concatenate(groups, axis=0)
        if k + 1 < NB:
            upper = work[lo:hi, hi:]
            lower = dot_full(work[hi:N, lo:hi], pivot)
            work[hi:N, hi:] -= dot_full(lower, upper)
            work[hi:N, lo:hi] = lower
        gain = dot_split(work[N:, lo:hi], pivot)
        if k + 1 < NB:
            work[N:, hi:] -= dot_split(gain, upper)
        work[N:, lo:hi] = gain


def first_kernel(meta, *refs):
    pieces, columns = refs[:2 * CHIPS], refs[2 * CHIPS:3 * CHIPS]
    begun, work = refs[3 * CHIPS:]
    for step in range(CHIPS):
        quarter = behind(meta[0], step)
        for other in range(2):
            place = quarter * 32 + (meta[3] if other == 0 else 1 - meta[3]) * 16
            for slot in range(NB):
                start = pl.multiple_of(slot * BLOCK + place, 16)
                for turn in range(TURNS):
                    col = (slot + turn) % NB
                    work[pl.ds(start, 16), col * BLOCK:(col + 1) * BLOCK] = pieces[2 * step + other][
                        slot, :, turn * BLOCK:(turn + 1) * BLOCK]
        for half in range(2):
            start = pl.multiple_of(N + half * BLOCK + quarter * 32, 32)
            work[pl.ds(start, 32), :] = columns[step][half * 32:(half + 1) * 32, :]
    for slot in range(NB):
        for turn in range(1, TURNS):
            col = (slot + turn) % NB
            work[col * BLOCK:(col + 1) * BLOCK, slot * BLOCK:(slot + 1) * BLOCK] = work[
                slot * BLOCK:(slot + 1) * BLOCK, col * BLOCK:(col + 1) * BLOCK].T
    lane = lax.broadcasted_iota(jnp.int32, (8, BLOCK), 1)
    sub = lax.broadcasted_iota(jnp.int32, (8, BLOCK), 0)
    eliminate(work, range(CUT), lane, sub)
    begun[...] = work[...]


def second_kernel(meta, begun, gain_ref, work):
    work[...] = begun[...]
    lane = lax.broadcasted_iota(jnp.int32, (8, BLOCK), 1)
    sub = lax.broadcasted_iota(jnp.int32, (8, BLOCK), 0)
    eliminate(work, range(CUT, NB), lane, sub)
    gain_ref[:, N - BLOCK:] = work[N:, N - BLOCK:].astype(gain_ref.dtype)
    for k in range(NB - 2, -1, -1):
        lo, hi = k * BLOCK, (k + 1) * BLOCK
        work[N:, lo:hi] -= dot_split(work[N:, hi:], work[hi:N, lo:hi])
        gain_ref[:, lo:hi] = work[N:, lo:hi].astype(gain_ref.dtype)


def solve_first(meta, pieces, columns):
    extra = CHIPS * columns[0].shape[0]
    return pl.pallas_call(
        first_kernel,
        out_shape=shape((N + extra, N), F32),
        in_specs=[SMEM] + whole(3 * CHIPS),
        out_specs=pl.BlockSpec(memory_space=pltpu.VMEM),
        scratch_shapes=[pltpu.VMEM((N + extra, N), F32)],
        compiler_params=params(28),
        cost_estimate=cost(3 * 10**10, 10**7),
    )(meta, *pieces, *columns)


def solve_second(meta, begun):
    return pl.pallas_call(
        second_kernel,
        out_shape=shape((begun.shape[0] - N, N), BF16),
        in_specs=[SMEM] + whole(1),
        out_specs=pl.BlockSpec(memory_space=pltpu.VMEM),
        scratch_shapes=[pltpu.VMEM(begun.shape, F32)],
        compiler_params=params(28),
        cost_estimate=cost(3 * 10**10, 10**7),
    )(meta, begun)


def rows_kernel(meta, weight_ref, *refs):
    outs, keep_ref, send_ref = refs[:CHIPS], refs[CHIPS], refs[CHIPS + 1]
    width = weight_ref.shape[1] // 2
    for step in range(CHIPS):
        quarter = ahead(meta[2], step)
        for half in range(2):
            start = pl.multiple_of(half * BLOCK + quarter * 32, 32)
            outs[step][half] = weight_ref[pl.ds(start, 32), :]
    keep_ref[...] = weight_ref[:, pl.ds(pl.multiple_of(meta[3] * width, BLOCK), width)]
    send_ref[...] = weight_ref[:, pl.ds(pl.multiple_of((1 - meta[3]) * width, BLOCK), width)]


def weight_rows(meta, weight):
    rows, width = weight.shape
    return pl.pallas_call(
        rows_kernel,
        out_shape=[shape((2, 32, width), BF16)] * CHIPS + [shape((rows, width // 2), BF16)] * 2,
        in_specs=[SMEM] + whole(1),
        out_specs=whole(CHIPS + 2),
        compiler_params=params(),
        cost_estimate=cost(10**6, 4 * 10**6),
    )(meta, weight)


def choose_weight_kernel(meta, a, b, c, d, keep_ref, send_ref):
    width = keep_ref.shape[2]
    keep_at = pl.ds(pl.multiple_of(meta[3] * width, BLOCK), width)
    send_at = pl.ds(pl.multiple_of((1 - meta[3]) * width, BLOCK), width)
    for slot in range(NB):
        y, step, core, half = source_of(meta, slot)
        mine = jnp.logical_and(y == meta[1], core == meta[3])
        keep_ref[slot] = jnp.zeros(keep_ref.shape[1:], BF16)
        send_ref[slot] = jnp.zeros(keep_ref.shape[1:], BF16)
        for index, part in enumerate((a, b, c, d)):
            @pl.when(jnp.logical_and(mine, step == index))
            def _(part=part):
                keep_ref[slot] = part[half, :, keep_at]
                send_ref[slot] = part[half, :, send_at]


def chosen_weight(meta, parts):
    width = parts[0].shape[2] // 2
    return pl.pallas_call(
        choose_weight_kernel,
        out_shape=[shape((NB, 32, width), BF16)] * 2,
        in_specs=[SMEM] + whole(CHIPS),
        out_specs=whole(2),
        compiler_params=params(),
        cost_estimate=cost(10**6, 2 * 10**6),
    )(meta, *parts)


def update_rows(meta, place, gain_ref, kept, before_ref, out_ref):
    keeps = []
    for half in range(2):
        number = ((meta[1] * CHIPS + meta[2]) * 2 + place) * 2 + half
        keep = jnp.float32(1.0)
        for slot in range(NB):
            keep = jnp.where(block_number(meta, slot) == number, 0.0, keep)
        keeps.append(keep)
    for col in range(0, out_ref.shape[1], 256):
        update = jnp.dot(gain_ref[...], kept[:, col:col + 256], preferred_element_type=F32)
        for half in range(2):
            rows = slice(half * BLOCK, (half + 1) * BLOCK)
            before = before_ref[rows, col:col + 256].astype(F32)
            out_ref[rows, col:col + 256] = ((before - update[rows]) * keeps[half]).astype(BF16)


def own_update_kernel(meta, gain_ref, *refs):
    parts, (before_ref, out_ref, kept) = refs[:CHIPS], refs[CHIPS:]
    for step in range(CHIPS):
        row = behind(meta[2], step)
        for slot in range(NB):
            start = pl.multiple_of(slot * BLOCK + row * 32, 32)
            kept[pl.ds(start, 32), :] = parts[step][slot]
    update_rows(meta, meta[3], gain_ref, kept, before_ref, out_ref)


def other_update_kernel(meta, gain_ref, kept, before_ref, out_ref):
    update_rows(meta, 1 - meta[3], gain_ref, kept, before_ref, out_ref)


def updated_own(meta, gain, kept_parts, before):
    return pl.pallas_call(
        own_update_kernel,
        out_shape=[shape(before.shape, BF16), shape((N, before.shape[1]), BF16)],
        in_specs=[SMEM] + whole(CHIPS + 2),
        out_specs=whole(2),
        compiler_params=params(),
        cost_estimate=cost(10**9, 6 * 10**6),
    )(meta, gain, *kept_parts, before)


def updated_other(meta, gain, kept, before):
    return pl.pallas_call(
        other_update_kernel,
        out_shape=shape(before.shape, BF16),
        in_specs=[SMEM] + whole(3),
        out_specs=pl.BlockSpec(memory_space=pltpu.VMEM),
        compiler_params=params(),
        cost_estimate=cost(10**9, 4 * 10**6),
    )(meta, gain, kept, before)


def dot_last(a, b):
    return lax.dot_general(a, b, (((1,), (1,)), ((), ())), preferred_element_type=F32)


def project_kernel(meta, tokens_ref, own_left, own_right, other_left, other_right, out_ref):
    rows, width = own_left.shape
    core = meta[3]
    left = tokens_ref[:, pl.ds(pl.multiple_of(core * width, BLOCK), width)]
    right = tokens_ref[:, pl.ds(pl.multiple_of((1 - core) * width, BLOCK), width)]
    own_at = pl.ds(pl.multiple_of(core * rows, rows), rows)
    other_at = pl.ds(pl.multiple_of((1 - core) * rows, rows), rows)
    out_ref[own_at, :] = (
        dot_last(own_left[...], left) + dot_last(own_right[...], right)
    ).astype(out_ref.dtype)
    out_ref[other_at, :] = (
        dot_last(other_left[...], left) + dot_last(other_right[...], right)
    ).astype(out_ref.dtype)


def projected(meta, tokens, parts, step, dtype):
    count, width = tokens.shape[0] // CHIPS, tokens.shape[1]
    rows = parts[0].shape[0]
    full = pl.BlockSpec(parts[0].shape, lambda i, meta: (0, 0))
    return pl.pallas_call(
        project_kernel,
        out_shape=shape((2 * rows, count), dtype),
        grid_spec=pltpu.PrefetchScalarGridSpec(
            num_scalar_prefetch=1,
            grid=(1,),
            in_specs=[pl.BlockSpec((count, width), lambda i, meta: (ahead(meta[0], step), 0))]
            + [full] * 4,
            out_specs=pl.BlockSpec((2 * rows, count), lambda i, meta: (0, 0)),
        ),
        compiler_params=params(),
        cost_estimate=cost(10**9, 4 * 10**6),
    )(meta, tokens, *parts)


def gram_kernel(mirror, meta, *refs):
    own, first, second = refs[:CHIPS], refs[CHIPS:2 * CHIPS], refs[2 * CHIPS:3 * CHIPS]
    out_ref, left = refs[3 * CHIPS:]
    x, y, z, core = meta[0], meta[1], meta[2], meta[3]
    rows = pl.ds(pl.multiple_of((1 - core if mirror else core) * 256, 256), 256)
    for step in range(CHIPS):
        at = lax.rem(y - x + step + CHIPS, CHIPS)
        left[:, pl.ds(pl.multiple_of(at * BLOCK, BLOCK), BLOCK)] = own[step][rows, :BLOCK]
        left[:, pl.ds(pl.multiple_of((at + CHIPS) * BLOCK, BLOCK), BLOCK)] = own[step][rows, BLOCK:]
    width = first[0].shape[1]
    for step in range(CHIPS):
        right = jnp.concatenate(
            [first[back][step] for back in range(CHIPS)]
            + [second[step][back] for back in range(CHIPS)], axis=1)
        at = pl.multiple_of(behind(z, step) * width, width)
        out_ref[:, pl.ds(at, width)] = lax.dot_general(
            left[...], right, (((1,), (1,)), ((), ())), preferred_element_type=F32
        ).astype(out_ref.dtype)


def gram_rows(meta, own, first, second, mirror, dtype):
    rows, width = 256, first[0].shape[1] * CHIPS
    return pl.pallas_call(
        lambda *refs: gram_kernel(mirror, *refs),
        out_shape=shape((rows, width), dtype),
        in_specs=[SMEM] + whole(3 * CHIPS),
        out_specs=pl.BlockSpec(memory_space=pltpu.VMEM),
        scratch_shapes=[pltpu.VMEM((rows, 2 * CHIPS * BLOCK), BF16)],
        compiler_params=params(),
        cost_estimate=cost(2 * 10**9, 6 * 10**6),
    )(meta, *own, *first, *second)


def device_id(x, y, z, c):
    return ((y * CHIPS + z) * 2 + c) * CHIPS + x


def permute(value, target):
    pairs = []
    for x in range(CHIPS):
        for y in range(CHIPS):
            for z in range(CHIPS):
                for c in range(2):
                    pairs.append((device_id(x, y, z, c), device_id(*target(x, y, z, c))))
    return lax.ppermute(value, AXES, pairs)


def shifted(value, axis, step):
    def target(x, y, z, c):
        at = [x, y, z, c]
        at[axis] = (at[axis] + step) % CHIPS
        return at

    return permute(value, target)


def partner(value):
    return permute(value, lambda x, y, z, c: (x, y, z, 1 - c))


def gathered(value, axis):
    far, near, back = (shifted(value, axis, step) for step in (2, 1, 3))
    return [value, near, far, back]


def exchanged(parts, axis):
    far, near, back = (shifted(parts[step], axis, step) for step in (2, 1, 3))
    return [parts[0], near, far, back]


def after(value, *others):
    return lax.optimization_barrier((value,) + others)[0]


def shards(calib, weight, inverse_factor, pruned_blocks):
    rows_dev, width_dev = weight.shape
    full_width = width_dev * CHIPS
    r = lax.axis_index("rows")
    x = lax.axis_index("mp")
    core = lax.rem(r, 2)
    meta = jnp.concatenate(
        [jnp.stack([x, lax.div(r, 8), lax.rem(lax.div(r, 2), CHIPS), core]), pruned_blocks]
    ).astype(jnp.int32)
    token_count = calib.shape[0] * 32

    plane = [[core_at + 2 * chip for chip in range(16)] for core_at in range(2)]
    tokens = lax.all_gather(calib, "rows", axis=0, tiled=True, axis_index_groups=plane)

    sums = exchanged(pruned_columns(meta, inverse_factor), 0)
    *cut, own_weight, send_weight = weight_rows(meta, weight)
    columns, keep, send = turned_rows(after(meta, own_weight), sums)
    cut = exchanged(cut, 2)
    line = gathered(jnp.stack([keep, partner(send)]), 2)
    columns = gathered(columns, 0)
    parts = gathered(chosen_rows(after(meta, *cut), line), 1)
    parts[0] = after(parts[0], *columns)
    total = (parts[0] + parts[1]) + (parts[2] + parts[3])
    pieces = []
    for piece in lax.optimization_barrier(tuple(gathered(total, 0))):
        pieces += [piece, partner(piece)]

    other_weight = partner(send_weight)
    keep, send = chosen_weight(after(meta, pieces[0]), cut)
    kept_line = keep + partner(send)
    begun = solve_first(after(meta, kept_line), pieces, columns)
    kept_sums = gathered(kept_line, 1)
    kept_quarter = (kept_sums[0] + kept_sums[1]) + (kept_sums[2] + kept_sums[3])
    gain = solve_second(after(meta, kept_quarter), begun)
    kept_parts = gathered(kept_quarter, 2)

    own_left, kept = updated_own(after(meta, gain, tokens), gain, kept_parts, own_weight)
    other_left = updated_other(meta, partner(gain), kept, other_weight)
    other_right, own_right = partner(own_left), partner(other_left)
    pruned_weight = jnp.where(
        core == 0,
        jnp.concatenate([own_left, own_right], axis=1),
        jnp.concatenate([own_right, own_left], axis=1),
    )

    sides = [own_left, own_right, other_left, other_right]
    sends = {step: projected(meta, tokens, sides, step, BF16) for step in (2, 1, 3)}
    got = [shifted(sends[step], 0, step) for step in (2, 1, 3)]
    summed = projected(meta, tokens, sides, 0, F32)
    for value in got:
        summed = summed + value.astype(F32)
    chunk = (summed * float(full_width) ** (-0.5)).astype(BF16)

    crossed = [
        permute(part, lambda x, y, z, c: (y, x, z, c)) for part in (chunk[:, :BLOCK], chunk[:, BLOCK:])
    ]
    crossed = lax.optimization_barrier(tuple(crossed))
    by_z = jnp.stack(gathered(crossed[0], 2))
    by_y = jnp.stack(gathered(crossed[1], 1))
    own = gathered(after(chunk, *crossed), 0)
    by_z, by_y, *own = lax.optimization_barrier((by_z, by_y, *own))
    first = gathered(by_z, 1)
    second = gathered(by_y, 2)
    given = partner(gram_rows(after(meta, pruned_weight), own, first, second, True, BF16))
    gram_block = (gram_rows(meta, own, first, second, False, F32) + given.astype(F32)) / token_count
    return (pruned_weight, gram_block)


def solution(mesh):
    return jax.shard_map(
        shards,
        mesh=mesh,
        in_specs=(P("rows", "mp"), P("rows", "mp"), P("rows", "mp"), P()),
        out_specs=(P("rows", "mp"), P("rows", "mp")),
        check_vma=False,
    )
```

```python
import jax
import jax.numpy as jnp
from jax import lax
from jax.experimental import pallas as pl
from jax.experimental.pallas import tpu as pltpu
from jax.sharding import PartitionSpec as P

BLOCK = 128
NB = 7
F32 = jnp.float32
GROUPS = BLOCK // 8
PANEL = 4


def dot_full(a, b):
    return lax.dot_general(
        a, b, (((1,), (0,)), ((), ())), precision=lax.Precision.HIGHEST, preferred_element_type=F32
    )


def dot_once(a, b):
    return lax.dot_general(a, b, (((1,), (0,)), ((), ())), preferred_element_type=F32)


def halves(a):
    high = a.astype(jnp.bfloat16)
    return high, (a - high.astype(F32)).astype(jnp.bfloat16)


def dot_split(a, b):
    (a_high, a_low), (b_high, b_low) = halves(a), halves(b)
    return dot_once(a_high, b_high) + (dot_once(a_high, b_low) + dot_once(a_low, b_high))


def spread(v):
    return jnp.broadcast_to(v, (8, BLOCK))


def lane_of(v, k):
    return jnp.take_along_axis(v, jnp.full((8, BLOCK), k, jnp.int32), axis=1)


def tree(terms):
    while len(terms) > 1:
        terms = [
            terms[i] + terms[i + 1] if i + 1 < len(terms) else terms[i]
            for i in range(0, len(terms), 2)
        ]
    return terms[0]


def invert_small(e):
    n = len(e)
    if n == 2:
        a, b, d = e[0][0], e[0][1], e[1][1]
        r = 1.0 / (a * d - b * b)
        off = -(b * r)
        return [[d * r, off], [off, a * r]]
    h = n // 2
    p = invert_small([row[:h] for row in e[:h]])
    b = [row[h:] for row in e[:h]]
    w = [[tree([p[i][k] * b[k][j] for k in range(h)]) for j in range(h)] for i in range(h)]
    s = [[None] * h for _ in range(h)]
    for i in range(h):
        for j in range(i, h):
            s[i][j] = s[j][i] = e[h + i][h + j] - tree([b[k][i] * w[k][j] for k in range(h)])
    t = invert_small(s)
    v = [[tree([w[i][k] * t[k][j] for k in range(h)]) for j in range(h)] for i in range(h)]
    q = [[None] * n for _ in range(n)]
    for i in range(h):
        for j in range(h):
            q[h + i][h + j] = t[i][j]
            q[i][h + j] = q[h + j][i] = -v[i][j]
        for j in range(i, h):
            q[i][j] = q[j][i] = p[i][j] + tree([v[i][k] * w[j][k] for k in range(h)])
    return q


def panel_steps(groups, first, lane, sub):
    for home in range(len(groups)):
        k = first + 8 * home
        cols = [[lane_of(group, k + t) for t in range(8)] for group in groups]
        e = [[None] * 8 for _ in range(8)]
        for t in range(8):
            for s in range(t + 1):
                e[s][t] = e[t][s] = spread(cols[home][t][s:s + 1, :])
        q = invert_small(e)
        inside = (lane >= k) & (lane < k + 8)
        rows = [
            jnp.where(lane == k + t, 1.0, jnp.where(inside, 0.0, spread(groups[home][t:t + 1, :])))
            for t in range(8)
        ]
        new = [tree([q[t][i] * rows[i] for i in range(8)]) for t in range(8)]
        out = []
        for g, group in enumerate(groups):
            if g == home:
                v = new[0]
                for t in range(1, 8):
                    v = jnp.where(sub == t, new[t], v)
            else:
                v = jnp.where(inside, 0.0, group) - tree([cols[g][t] * new[t] for t in range(8)])
            out.append(v)
        groups = out
    return groups


def invert_block(groups, lane, sub):
    for first in range(0, GROUPS, PANEL):
        panel = panel_steps(groups[first:first + PANEL], first * 8, lane, sub)
        inside = (lane >= first * 8) & (lane < (first + PANEL) * 8)
        left = jnp.concatenate(groups, axis=0)[:, first * 8:(first + PANEL) * 8]
        change = dot_full(left, jnp.concatenate(panel, axis=0))
        groups = [
            panel[g - first]
            if first <= g < first + PANEL
            else jnp.where(inside, 0.0, groups[g]) - change[g * 8:g * 8 + 8, :]
            for g in range(GROUPS)
        ]
    return groups


CHIPS = 4
TURNS = NB // 2 + 1
AXES = ("rows", "mp")
N = NB * BLOCK
BF16 = jnp.bfloat16
META = 4
CUT = 4


def whole(count):
    return [pl.BlockSpec(memory_space=pltpu.VMEM)] * count


SMEM = pl.BlockSpec(memory_space=pltpu.SMEM)
ANY = pl.BlockSpec(memory_space=pl.ANY)


def cost(flops, data):
    return pl.CostEstimate(flops=flops, bytes_accessed=data, transcendentals=0)


def params(mebibytes=16):
    return pltpu.CompilerParams(vmem_limit_bytes=mebibytes * 2**20)


def shape(dims, dtype):
    return jax.ShapeDtypeStruct(dims, dtype)


def ahead(place, step):
    return lax.rem(place + step, CHIPS)


def behind(place, step):
    return lax.rem(place - step + CHIPS, CHIPS)


def block_number(meta, slot):
    return meta[META + slot]


def columns_kernel(meta, source, *refs):
    outs, buffer, sems = refs[:CHIPS], refs[CHIPS], refs[CHIPS + 1]
    width = source.shape[1]
    inside = []
    for slot in range(NB):
        offset = block_number(meta, slot) * BLOCK - meta[0] * width
        ok = jnp.logical_and(offset >= 0, offset < width)
        inside.append(jnp.where(ok, 1.0, 0.0).astype(F32))
        start = pl.multiple_of(jnp.clip(offset, 0, width - BLOCK), BLOCK)
        pltpu.make_async_copy(source.at[:, pl.ds(start, BLOCK)], buffer.at[slot], sems.at[slot]).start()
    for slot in range(NB):
        pltpu.make_async_copy(source.at[:, pl.ds(0, BLOCK)], buffer.at[slot], sems.at[slot]).wait()
        for step in range(CHIPS):
            quarter = ahead(meta[0], step)
            for half in range(2):
                start = pl.multiple_of(half * BLOCK + quarter * 32, 32)
                outs[step][half, :, slot * BLOCK:(slot + 1) * BLOCK] = (
                    buffer[slot, pl.ds(start, 32), :] * inside[slot]
                )


def pruned_columns(meta, inverse_factor):
    return pl.pallas_call(
        columns_kernel,
        out_shape=[shape((2, 32, N), F32)] * CHIPS,
        in_specs=[SMEM, ANY],
        out_specs=whole(CHIPS),
        scratch_shapes=[
            pltpu.VMEM((NB, inverse_factor.shape[0], BLOCK), F32),
            pltpu.SemaphoreType.DMA((NB,)),
        ],
        compiler_params=params(),
        cost_estimate=cost(10**6, 6 * 10**6),
    )(meta, inverse_factor)


def turn_kernel(meta, a, b, c, d, columns_ref, keep_ref, send_ref, doubled):
    core = meta[3]
    number = (meta[1] * CHIPS + meta[2]) * 2 + core
    for half in range(2):
        total = (a[half] + b[half]) + (c[half] + d[half])
        columns_ref[half * 32:(half + 1) * 32, :] = total
        doubled[half * 32:(half + 1) * 32, :N] = total
        doubled[half * 32:(half + 1) * 32, N:] = total[:, :(TURNS - 1) * BLOCK]
    for half in range(2):
        slot = jnp.int32(0)
        for candidate in range(NB):
            slot = jnp.where(block_number(meta, candidate) == 2 * number + half, candidate, slot)
        lanes = pl.ds(pl.multiple_of(slot * BLOCK, BLOCK), TURNS * BLOCK)
        keep_ref[half] = doubled[pl.ds(pl.multiple_of(half * 32 + core * 16, 16), 16), lanes]
        send_ref[half] = doubled[pl.ds(pl.multiple_of(half * 32 + (1 - core) * 16, 16), 16), lanes]


def turned_rows(meta, parts):
    return pl.pallas_call(
        turn_kernel,
        out_shape=[shape((64, N), F32)] + [shape((2, 16, TURNS * BLOCK), F32)] * 2,
        in_specs=[SMEM] + whole(CHIPS),
        out_specs=whole(3),
        scratch_shapes=[pltpu.VMEM((64, N + (TURNS - 1) * BLOCK), F32)],
        compiler_params=params(),
        cost_estimate=cost(10**6, 2 * 10**6),
    )(meta, *parts)


def source_of(meta, slot):
    block = block_number(meta, slot)
    y, z = lax.div(block, 16), lax.rem(lax.div(block, 4), 4)
    return y, behind(meta[2], z), lax.rem(lax.div(block, 2), 2), lax.rem(block, 2)


def choose_kernel(meta, a, b, c, d, out_ref):
    for slot in range(NB):
        y, step, core, half = source_of(meta, slot)
        apart = jnp.where(core == meta[3], 0, 1)
        out_ref[slot] = jnp.zeros(out_ref.shape[1:], out_ref.dtype)
        for index, part in enumerate((a, b, c, d)):
            @pl.when(jnp.logical_and(y == meta[1], step == index))
            def _(part=part):
                out_ref[slot] = part[apart, half]


def chosen_rows(meta, parts):
    return pl.pallas_call(
        choose_kernel,
        out_shape=shape((NB, 16, TURNS * BLOCK), F32),
        in_specs=[SMEM] + whole(CHIPS),
        out_specs=pl.BlockSpec(memory_space=pltpu.VMEM),
        compiler_params=params(),
        cost_estimate=cost(10**6, 10**6),
    )(meta, *parts)


def eliminate(work, numbers, lane, sub):
    for k in numbers:
        lo, hi = k * BLOCK, (k + 1) * BLOCK
        groups = invert_block([work[lo + g * 8:lo + g * 8 + 8, lo:hi] for g in range(GROUPS)], lane, sub)
        pivot = jnp.concatenate(groups, axis=0)
        if k + 1 < NB:
            upper = work[lo:hi, hi:]
            lower = dot_full(work[hi:N, lo:hi], pivot)
            work[hi:N, hi:] -= dot_full(lower, upper)
            work[hi:N, lo:hi] = lower
        gain = dot_split(work[N:, lo:hi], pivot)
        if k + 1 < NB:
            work[N:, hi:] -= dot_split(gain, upper)
        work[N:, lo:hi] = gain


def first_kernel(meta, *refs):
    pieces, columns = refs[:2 * CHIPS], refs[2 * CHIPS:3 * CHIPS]
    begun, work = refs[3 * CHIPS:]
    for step in range(CHIPS):
        quarter = behind(meta[0], step)
        for other in range(2):
            place = quarter * 32 + (meta[3] if other == 0 else 1 - meta[3]) * 16
            for slot in range(NB):
                start = pl.multiple_of(slot * BLOCK + place, 16)
                for turn in range(TURNS):
                    col = (slot + turn) % NB
                    work[pl.ds(start, 16), col * BLOCK:(col + 1) * BLOCK] = pieces[2 * step + other][
                        slot, :, turn * BLOCK:(turn + 1) * BLOCK]
        for half in range(2):
            start = pl.multiple_of(N + half * BLOCK + quarter * 32, 32)
            work[pl.ds(start, 32), :] = columns[step][half * 32:(half + 1) * 32, :]
    for slot in range(NB):
        for turn in range(1, TURNS):
            col = (slot + turn) % NB
            work[col * BLOCK:(col + 1) * BLOCK, slot * BLOCK:(slot + 1) * BLOCK] = work[
                slot * BLOCK:(slot + 1) * BLOCK, col * BLOCK:(col + 1) * BLOCK].T
    lane = lax.broadcasted_iota(jnp.int32, (8, BLOCK), 1)
    sub = lax.broadcasted_iota(jnp.int32, (8, BLOCK), 0)
    eliminate(work, range(CUT), lane, sub)
    begun[...] = work[...]


def second_kernel(meta, begun, gain_ref, work):
    work[...] = begun[...]
    lane = lax.broadcasted_iota(jnp.int32, (8, BLOCK), 1)
    sub = lax.broadcasted_iota(jnp.int32, (8, BLOCK), 0)
    eliminate(work, range(CUT, NB), lane, sub)
    gain_ref[:, N - BLOCK:] = work[N:, N - BLOCK:].astype(gain_ref.dtype)
    for k in range(NB - 2, -1, -1):
        lo, hi = k * BLOCK, (k + 1) * BLOCK
        work[N:, lo:hi] -= dot_split(work[N:, hi:], work[hi:N, lo:hi])
        gain_ref[:, lo:hi] = work[N:, lo:hi].astype(gain_ref.dtype)


def solve_first(meta, pieces, columns):
    extra = CHIPS * columns[0].shape[0]
    return pl.pallas_call(
        first_kernel,
        out_shape=shape((N + extra, N), F32),
        in_specs=[SMEM] + whole(3 * CHIPS),
        out_specs=pl.BlockSpec(memory_space=pltpu.VMEM),
        scratch_shapes=[pltpu.VMEM((N + extra, N), F32)],
        compiler_params=params(28),
        cost_estimate=cost(3 * 10**10, 10**7),
    )(meta, *pieces, *columns)


def solve_second(meta, begun):
    return pl.pallas_call(
        second_kernel,
        out_shape=shape((begun.shape[0] - N, N), BF16),
        in_specs=[SMEM] + whole(1),
        out_specs=pl.BlockSpec(memory_space=pltpu.VMEM),
        scratch_shapes=[pltpu.VMEM(begun.shape, F32)],
        compiler_params=params(28),
        cost_estimate=cost(3 * 10**10, 10**7),
    )(meta, begun)


def rows_kernel(meta, weight_ref, *refs):
    outs, keep_ref, send_ref = refs[:CHIPS], refs[CHIPS], refs[CHIPS + 1]
    width = weight_ref.shape[1] // 2
    for step in range(CHIPS):
        quarter = ahead(meta[2], step)
        for half in range(2):
            start = pl.multiple_of(half * BLOCK + quarter * 32, 32)
            outs[step][half] = weight_ref[pl.ds(start, 32), :]
    keep_ref[...] = weight_ref[:, pl.ds(pl.multiple_of(meta[3] * width, BLOCK), width)]
    send_ref[...] = weight_ref[:, pl.ds(pl.multiple_of((1 - meta[3]) * width, BLOCK), width)]


def weight_rows(meta, weight):
    rows, width = weight.shape
    return pl.pallas_call(
        rows_kernel,
        out_shape=[shape((2, 32, width), BF16)] * CHIPS + [shape((rows, width // 2), BF16)] * 2,
        in_specs=[SMEM] + whole(1),
        out_specs=whole(CHIPS + 2),
        compiler_params=params(),
        cost_estimate=cost(10**6, 4 * 10**6),
    )(meta, weight)


def choose_weight_kernel(meta, a, b, c, d, keep_ref, send_ref):
    width = keep_ref.shape[2]
    keep_at = pl.ds(pl.multiple_of(meta[3] * width, BLOCK), width)
    send_at = pl.ds(pl.multiple_of((1 - meta[3]) * width, BLOCK), width)
    for slot in range(NB):
        y, step, core, half = source_of(meta, slot)
        mine = jnp.logical_and(y == meta[1], core == meta[3])
        keep_ref[slot] = jnp.zeros(keep_ref.shape[1:], BF16)
        send_ref[slot] = jnp.zeros(keep_ref.shape[1:], BF16)
        for index, part in enumerate((a, b, c, d)):
            @pl.when(jnp.logical_and(mine, step == index))
            def _(part=part):
                keep_ref[slot] = part[half, :, keep_at]
                send_ref[slot] = part[half, :, send_at]


def chosen_weight(meta, parts):
    width = parts[0].shape[2] // 2
    return pl.pallas_call(
        choose_weight_kernel,
        out_shape=[shape((NB, 32, width), BF16)] * 2,
        in_specs=[SMEM] + whole(CHIPS),
        out_specs=whole(2),
        compiler_params=params(),
        cost_estimate=cost(10**6, 2 * 10**6),
    )(meta, *parts)


def update_rows(meta, place, gain_ref, kept, before_ref, out_ref):
    keeps = []
    for half in range(2):
        number = ((meta[1] * CHIPS + meta[2]) * 2 + place) * 2 + half
        keep = jnp.float32(1.0)
        for slot in range(NB):
            keep = jnp.where(block_number(meta, slot) == number, 0.0, keep)
        keeps.append(keep)
    for col in range(0, out_ref.shape[1], 256):
        update = jnp.dot(gain_ref[...], kept[:, col:col + 256], preferred_element_type=F32)
        for half in range(2):
            rows = slice(half * BLOCK, (half + 1) * BLOCK)
            before = before_ref[rows, col:col + 256].astype(F32)
            out_ref[rows, col:col + 256] = ((before - update[rows]) * keeps[half]).astype(BF16)


def own_update_kernel(meta, gain_ref, *refs):
    parts, (before_ref, out_ref, kept) = refs[:CHIPS], refs[CHIPS:]
    for step in range(CHIPS):
        row = behind(meta[2], step)
        for slot in range(NB):
            start = pl.multiple_of(slot * BLOCK + row * 32, 32)
            kept[pl.ds(start, 32), :] = parts[step][slot]
    update_rows(meta, meta[3], gain_ref, kept, before_ref, out_ref)


def other_update_kernel(meta, gain_ref, kept, before_ref, out_ref):
    update_rows(meta, 1 - meta[3], gain_ref, kept, before_ref, out_ref)


def updated_own(meta, gain, kept_parts, before):
    return pl.pallas_call(
        own_update_kernel,
        out_shape=[shape(before.shape, BF16), shape((N, before.shape[1]), BF16)],
        in_specs=[SMEM] + whole(CHIPS + 2),
        out_specs=whole(2),
        compiler_params=params(),
        cost_estimate=cost(10**9, 6 * 10**6),
    )(meta, gain, *kept_parts, before)


def updated_other(meta, gain, kept, before):
    return pl.pallas_call(
        other_update_kernel,
        out_shape=shape(before.shape, BF16),
        in_specs=[SMEM] + whole(3),
        out_specs=pl.BlockSpec(memory_space=pltpu.VMEM),
        compiler_params=params(),
        cost_estimate=cost(10**9, 4 * 10**6),
    )(meta, gain, kept, before)


def dot_last(a, b):
    return lax.dot_general(a, b, (((1,), (1,)), ((), ())), preferred_element_type=F32)


def project_kernel(meta, tokens_ref, own_left, own_right, other_left, other_right, out_ref):
    rows, width = own_left.shape
    core = meta[3]
    left = tokens_ref[:, pl.ds(pl.multiple_of(core * width, BLOCK), width)]
    right = tokens_ref[:, pl.ds(pl.multiple_of((1 - core) * width, BLOCK), width)]
    own_at = pl.ds(pl.multiple_of(core * rows, rows), rows)
    other_at = pl.ds(pl.multiple_of((1 - core) * rows, rows), rows)
    out_ref[own_at, :] = (
        dot_last(own_left[...], left) + dot_last(own_right[...], right)
    ).astype(out_ref.dtype)
    out_ref[other_at, :] = (
        dot_last(other_left[...], left) + dot_last(other_right[...], right)
    ).astype(out_ref.dtype)


def projected(meta, tokens, parts, step, dtype):
    count, width = tokens.shape[0] // CHIPS, tokens.shape[1]
    rows = parts[0].shape[0]
    full = pl.BlockSpec(parts[0].shape, lambda i, meta: (0, 0))
    return pl.pallas_call(
        project_kernel,
        out_shape=shape((2 * rows, count), dtype),
        grid_spec=pltpu.PrefetchScalarGridSpec(
            num_scalar_prefetch=1,
            grid=(1,),
            in_specs=[pl.BlockSpec((count, width), lambda i, meta: (ahead(meta[0], step), 0))]
            + [full] * 4,
            out_specs=pl.BlockSpec((2 * rows, count), lambda i, meta: (0, 0)),
        ),
        compiler_params=params(),
        cost_estimate=cost(10**9, 4 * 10**6),
    )(meta, tokens, *parts)


def gram_kernel(mirror, meta, *refs):
    own, first, second = refs[:CHIPS], refs[CHIPS:2 * CHIPS], refs[2 * CHIPS:3 * CHIPS]
    out_ref, left = refs[3 * CHIPS:]
    x, y, z, core = meta[0], meta[1], meta[2], meta[3]
    rows = pl.ds(pl.multiple_of((1 - core if mirror else core) * 256, 256), 256)
    for step in range(CHIPS):
        at = lax.rem(y - x + step + CHIPS, CHIPS)
        left[:, pl.ds(pl.multiple_of(at * BLOCK, BLOCK), BLOCK)] = own[step][rows, :BLOCK]
        left[:, pl.ds(pl.multiple_of((at + CHIPS) * BLOCK, BLOCK), BLOCK)] = own[step][rows, BLOCK:]
    width = first[0].shape[1]
    for step in range(CHIPS):
        right = jnp.concatenate(
            [first[back][step] for back in range(CHIPS)]
            + [second[step][back] for back in range(CHIPS)], axis=1)
        at = pl.multiple_of(behind(z, step) * width, width)
        out_ref[:, pl.ds(at, width)] = lax.dot_general(
            left[...], right, (((1,), (1,)), ((), ())), preferred_element_type=F32
        ).astype(out_ref.dtype)


def gram_rows(meta, own, first, second, mirror, dtype):
    rows, width = 256, first[0].shape[1] * CHIPS
    return pl.pallas_call(
        lambda *refs: gram_kernel(mirror, *refs),
        out_shape=shape((rows, width), dtype),
        in_specs=[SMEM] + whole(3 * CHIPS),
        out_specs=pl.BlockSpec(memory_space=pltpu.VMEM),
        scratch_shapes=[pltpu.VMEM((rows, 2 * CHIPS * BLOCK), BF16)],
        compiler_params=params(),
        cost_estimate=cost(2 * 10**9, 6 * 10**6),
    )(meta, *own, *first, *second)


def device_id(x, y, z, c):
    return ((y * CHIPS + z) * 2 + c) * CHIPS + x


def permute(value, target):
    pairs = []
    for x in range(CHIPS):
        for y in range(CHIPS):
            for z in range(CHIPS):
                for c in range(2):
                    pairs.append((device_id(x, y, z, c), device_id(*target(x, y, z, c))))
    return lax.ppermute(value, AXES, pairs)


def shifted(value, axis, step):
    def target(x, y, z, c):
        at = [x, y, z, c]
        at[axis] = (at[axis] + step) % CHIPS
        return at

    return permute(value, target)


def partner(value):
    return permute(value, lambda x, y, z, c: (x, y, z, 1 - c))


def gathered(value, axis):
    far, near, back = (shifted(value, axis, step) for step in (2, 1, 3))
    return [value, near, far, back]


def exchanged(parts, axis):
    far, near, back = (shifted(parts[step], axis, step) for step in (2, 1, 3))
    return [parts[0], near, far, back]


def after(value, *others):
    return lax.optimization_barrier((value,) + others)[0]


def shards(calib, weight, inverse_factor, pruned_blocks):
    rows_dev, width_dev = weight.shape
    full_width = width_dev * CHIPS
    r = lax.axis_index("rows")
    x = lax.axis_index("mp")
    core = lax.rem(r, 2)
    meta = jnp.concatenate(
        [jnp.stack([x, lax.div(r, 8), lax.rem(lax.div(r, 2), CHIPS), core]), pruned_blocks]
    ).astype(jnp.int32)
    token_count = calib.shape[0] * 32

    sums = exchanged(pruned_columns(meta, inverse_factor), 0)
    *cut, own_weight, send_weight = weight_rows(meta, weight)
    columns, keep, send = turned_rows(after(meta, own_weight), sums)
    cut = exchanged(cut, 2)
    line = gathered(jnp.stack([keep, partner(send)]), 2)
    columns = gathered(columns, 0)
    parts = gathered(chosen_rows(after(meta, *cut), line), 1)
    parts[0] = after(parts[0], *columns)
    total = (parts[0] + parts[1]) + (parts[2] + parts[3])
    pieces = []
    for piece in lax.optimization_barrier(tuple(gathered(total, 0))):
        pieces += [piece, partner(piece)]

    plane = [[core_at + 2 * chip for chip in range(16)] for core_at in range(2)]
    tokens = lax.all_gather(after(calib, total), "rows", axis=0, tiled=True, axis_index_groups=plane)

    other_weight = partner(send_weight)
    keep, send = chosen_weight(after(meta, pieces[0]), cut)
    kept_line = keep + partner(send)
    begun = solve_first(after(meta, kept_line), pieces, columns)
    kept_sums = gathered(kept_line, 1)
    kept_quarter = (kept_sums[0] + kept_sums[1]) + (kept_sums[2] + kept_sums[3])
    gain = solve_second(after(meta, kept_quarter), begun)
    kept_parts = gathered(kept_quarter, 2)

    own_left, kept = updated_own(after(meta, gain, tokens), gain, kept_parts, own_weight)
    other_left = updated_other(meta, partner(gain), kept, other_weight)
    other_right, own_right = partner(own_left), partner(other_left)
    pruned_weight = jnp.where(
        core == 0,
        jnp.concatenate([own_left, own_right], axis=1),
        jnp.concatenate([own_right, own_left], axis=1),
    )

    sides = [own_left, own_right, other_left, other_right]
    sends = {step: projected(meta, tokens, sides, step, BF16) for step in (2, 1, 3)}
    got = [shifted(sends[step], 0, step) for step in (2, 1, 3)]
    summed = projected(meta, tokens, sides, 0, F32)
    for value in got:
        summed = summed + value.astype(F32)
    chunk = (summed * float(full_width) ** (-0.5)).astype(BF16)

    crossed = [
        permute(part, lambda x, y, z, c: (y, x, z, c)) for part in (chunk[:, :BLOCK], chunk[:, BLOCK:])
    ]
    crossed = lax.optimization_barrier(tuple(crossed))
    by_z = jnp.stack(gathered(crossed[0], 2))
    by_y = jnp.stack(gathered(crossed[1], 1))
    own = gathered(after(chunk, *crossed), 0)
    by_z, by_y, *own = lax.optimization_barrier((by_z, by_y, *own))
    first = gathered(by_z, 1)
    second = gathered(by_y, 2)
    given = partner(gram_rows(after(meta, pruned_weight), own, first, second, True, BF16))
    gram_block = (gram_rows(meta, own, first, second, False, F32) + given.astype(F32)) / token_count
    return (pruned_weight, gram_block)


def solution(mesh):
    return jax.shard_map(
        shards,
        mesh=mesh,
        in_specs=(P("rows", "mp"), P("rows", "mp"), P("rows", "mp"), P()),
        out_specs=(P("rows", "mp"), P("rows", "mp")),
        check_vma=False,
    )
```
